128 devices in a mesh: dp: 16 (over z_hi, y, core), tensor: 8 (over x, z_lo).
Axes of the slice: x: 4, y: 4, z: 4 (z_hi: 2, z_lo: 2; z = z_hi * 2 + z_lo), core: 2. Of those that a mesh axis runs over, the one named last changes fastest.
Arguments:
- hidden_in: float32 [9728, 1024], P('dp'), may hold values from -6 to 6
- segments: int32 [16, 608], P('dp'), may hold values from 0 to 3, never falling along the last dimension, each value on 1 to 304 neighbouring positions
- ln1_gain: float32 [1024], replicated, may hold values from 0.1 to 1.9
- ln1_shift: float32 [1024], replicated, may hold values from -1.75 to 1.75
- qkv_weight: bfloat16 [1024, 3072], P(None, 'tensor'), may hold values from -0.1875 to 0.1875
- query_bias: float32 [1024], P('tensor'), may hold values from -3 to 3
- value_bias: float32 [1024], P('tensor'), may hold values from -3 to 3
- dense_weight: bfloat16 [1024, 1024], P('tensor'), may hold values from -0.75 to 0.75
- dense_bias: float32 [1024], replicated, may hold values from -3 to 3
- ln2_gain: float32 [1024], replicated, may hold values from 0.1 to 1.9
- ln2_shift: float32 [1024], replicated, may hold values from -1.75 to 1.75
- up_weight: bfloat16 [1024, 4096], P(None, 'tensor'), may hold values from -0.1875 to 0.1875
- up_bias: float32 [4096], P('tensor'), may hold values from -3 to 3
- down_weight: bfloat16 [4096, 1024], P('tensor'), may hold values from -0.125 to 0.125
- down_bias: float32 [1024], replicated, may hold values from -3 to 3
- out_grad: float32 [9728, 1024], P('dp'), may hold values from -6 to 6
Outputs:
- block_out: float32 [9728, 1024], P('dp')
- input_grad: float32 [9728, 1024], P('dp')
- ln1_gain_grad: float32 [1024], replicated
- ln1_shift_grad: float32 [1024], replicated
- qkv_weight_grad: float32 [1024, 3072], P(None, 'tensor')
- query_bias_grad: float32 [1024], P('tensor')
- value_bias_grad: float32 [1024], P('tensor')
- dense_weight_grad: float32 [1024, 1024], P('tensor')
- dense_bias_grad: float32 [1024], replicated
- ln2_gain_grad: float32 [1024], replicated
- ln2_shift_grad: float32 [1024], replicated
- up_weight_grad: float32 [1024, 4096], P(None, 'tensor')
- up_bias_grad: float32 [4096], P('tensor')
- down_weight_grad: float32 [4096, 1024], P('tensor')
- down_bias_grad: float32 [1024], replicated
The draws below stay inside these ranges and needn't reach their ends.
Inputs may be any that keep to these rules, and one draw needn't show every extreme that they name: `segments`: in each packed row the document numbers never fall and every number from 0 to 3 appears; documents hold 1 to 304 tokens, and every row has one of exactly 304.
All inputs are finite; a program needn't handle non-finite values.
Results may differ from the reference program's by a relative error of at most 0.012.
The reference program's roundings to bfloat16 on the way count: a program that leaves them out, or rounds other values in their place, can miss the bound.
Values may be sent and summed in bfloat16 or wider, within the bound.
No kernel may reach another device: no remote copies, remote signals or barrier semaphores. Data moves between devices by JAX's collectives and lax.ppermute only.
A program may use at most 128 MiB of HBM per device.

```python
import math
import jax
import jax.numpy as jnp
import numpy as np
from jax import lax

HEADS = 16
HEAD_DIM = 64
D = 1024
FF = 4096
SEQ = 608
ROWS = 16
TOKENS = 9728


def block_scale(own_key, extent, split, low, largest):
    def one(position, parts):
        steps = jax.random.uniform(jax.random.fold_in(jax.random.fold_in(own_key, 6), position), (parts,), jnp.float32, low / len(split), largest / len(split))
        return jnp.repeat(jnp.exp(steps), extent[position] // parts).reshape((-1,) + (1,) * (len(extent) - position - 1))

    level = one(*split[0])
    for cut in split[1:]:
        level = level * one(*cut)
    return level


def split_up(number_of, total, bound, slope):
    weights = [(1 << 20) // math.isqrt(standing ** slope) + 1 for standing in range(2, number_of + 1)]
    rest, given = total - bound - (number_of - 1), [1] * (number_of - 1)
    while rest > 0:
        candidates = [i for i in range(number_of - 1) if given[i] < bound]
        mass, budget = sum([weights[i] for i in candidates]), rest
        for i in candidates:
            more = min(bound - given[i], max(1, budget * weights[i] // mass), rest)
            given[i] = given[i] + more
            rest = rest - more
    return np.array([bound] + given)


def ragged_sizes(rng, amount, total, limit, lean):
    if amount == 2:
        one = jax.random.randint(rng, (), max(1, total - limit), min(limit, total - 1) + 1)
        return jnp.stack([one, total - one])
    tallies = jnp.asarray(split_up(amount, total, limit, lean), jnp.int32)
    couples = (amount - 1) // 2
    donor, receiver = tallies[1:1 + 2 * couples:2], tallies[2:2 + 2 * couples:2]
    slack = jnp.minimum(donor - 1, limit - receiver)
    moved = jax.random.randint(jax.random.fold_in(rng, 1), (couples,), 0, 1 << 20) % (slack + 1)
    tallies = tallies.at[1:1 + 2 * couples:2].set(donor - moved).at[2:2 + 2 * couples:2].set(receiver + moved)
    return tallies[jax.random.permutation(jax.random.fold_in(rng, 2), amount)]


def noise(stream_key, dims, width, bound, pieces=(), kind=jnp.bfloat16):
    array = jax.random.normal(stream_key, dims, jnp.float32) * width
    if len(pieces) > 0:
        array = block_scale(stream_key, dims, pieces, -0.22, 0.18) * array
    return jnp.clip(array, min=-bound, max=bound).astype(kind)


def setup_inputs(seed: int = 0) -> dict:
    arg_keys = jax.random.split(jax.random.key(seed), 17)
    return {
        "hidden_in": noise(arg_keys[0], (TOKENS, D), 1.0, 6.0, ((0, 16),), jnp.float32),
        "segments": jax.vmap(lambda own: jnp.searchsorted(jnp.cumsum(ragged_sizes(own, max(3, SEQ // 128), SEQ, SEQ // 2, 1)), jnp.arange(SEQ), side="right"))(jax.random.split(arg_keys[1], ROWS)).reshape((ROWS, SEQ)).astype(jnp.int32),
        "ln1_gain": jnp.clip(1.0 + 0.18 * jax.random.normal(arg_keys[2], (D,), jnp.float32), 0.1, 1.9),
        "ln1_shift": noise(arg_keys[3], (D,), 0.3, 1.75, (), jnp.float32),
        "qkv_weight": noise(arg_keys[4], (D, 3 * D), D ** -0.5, 0.1875, ((1, 8),)),
        "query_bias": noise(arg_keys[5], (D,), 0.5, 3.0, ((0, 8),), jnp.float32),
        "value_bias": noise(arg_keys[6], (D,), 0.5, 3.0, ((0, 8),), jnp.float32),
        "dense_weight": noise(arg_keys[7], (D, D), (D // 16) ** -0.5, 0.75, ((0, 8),)),
        "dense_bias": noise(arg_keys[8], (D,), 0.5, 3.0, (), jnp.float32),
        "ln2_gain": jnp.clip(1.0 + 0.18 * jax.random.normal(arg_keys[9], (D,), jnp.float32), 0.1, 1.9),
        "ln2_shift": noise(arg_keys[10], (D,), 0.3, 1.75, (), jnp.float32),
        "up_weight": noise(arg_keys[11], (D, FF), D ** -0.5, 0.1875, ((1, 8),)),
        "up_bias": noise(arg_keys[12], (FF,), 0.5, 3.0, ((0, 8),), jnp.float32),
        "down_weight": noise(arg_keys[13], (FF, D), (FF // 2) ** -0.5, 0.125, ((0, 8),)),
        "down_bias": noise(arg_keys[14], (D,), 0.5, 3.0, (), jnp.float32),
        "out_grad": noise(arg_keys[15], (TOKENS, D), 1.0, 6.0, ((0, 16),), jnp.float32),
    }


EPS = 1e-05
NEG = -1000000000.0

@jax.custom_vjp
def low(v):
    return lax.optimization_barrier(v.astype(jnp.bfloat16)).astype(jnp.float32)

@jax.custom_vjp
def low_back(v):
    return v

def low_keep(v):
    return (low(v), None)

def low_pass(kept, grad):
    return (grad,)

def back_keep(v):
    return (v, None)

def back_low(kept, grad):
    return (low(grad),)
low.defvjp(low_keep, low_pass)
low_back.defvjp(back_keep, back_low)

def layer_norm(values_in, gain_vec, shift_vec):
    row_mean = lax.optimization_barrier(jnp.mean(values_in, -1, keepdims=True))
    centred = values_in - row_mean
    variance = lax.optimization_barrier(jnp.mean(centred * centred, -1, keepdims=True))
    return centred * lax.rsqrt(variance + EPS) * gain_vec + shift_vec

def attend_row(queries, keys_all, values_all, segment_ids):
    length = queries.shape[0]
    positions = jnp.arange(length)
    distance = (positions[None, :] - positions[:, None]).astype(jnp.float32)
    allowed = (distance <= 0) & (segment_ids[:, None] == segment_ids[None, :])
    slopes = jnp.exp2(-(8.0 / HEADS) * (jnp.arange(HEADS) + 1).astype(jnp.float32))
    raw_scores = jnp.einsum('qhd,khd->hqk', queries, keys_all, precision=lax.Precision.HIGHEST) * HEAD_DIM ** (-0.5)
    raw_scores = raw_scores + slopes[:, None, None] * distance[None]
    raw_scores = low_back(jnp.where(allowed[None], raw_scores, NEG))
    probs = low(jax.nn.softmax(raw_scores, axis=-1))
    return jnp.einsum('hqk,khd->qhd', probs, values_all, precision=lax.Precision.HIGHEST)

def forward(hidden, gain_one, shift_one, w_qkv, bias_query, bias_value, w_dense, bias_dense, gain_two, shift_two, w_up, bias_up, w_down, bias_down, segments):
    high = lax.Precision.HIGHEST
    tokens_all = hidden.shape[0]
    row_count = tokens_all // SEQ
    normed1 = low(layer_norm(hidden, gain_one, shift_one))
    qkv_bias = jnp.stack([bias_query.reshape(HEADS, HEAD_DIM), jnp.zeros((HEADS, HEAD_DIM), jnp.float32), bias_value.reshape(HEADS, HEAD_DIM)], axis=1).reshape(-1)
    qkv = low(low_back(jnp.dot(normed1, w_qkv, precision=high) + qkv_bias))
    qkv = qkv.reshape(row_count, SEQ, HEADS, 3, HEAD_DIM)
    checked = jax.checkpoint(attend_row)
    context = lax.map(lambda row_item: checked(row_item[0], row_item[1], row_item[2], row_item[3]), (qkv[:, :, :, 0], qkv[:, :, :, 1], qkv[:, :, :, 2], segments))
    context = low(low_back(context.reshape(tokens_all, HEADS * HEAD_DIM)))
    middle = hidden + low_back(jnp.dot(context, w_dense, precision=high) + bias_dense)
    normed2 = low(layer_norm(middle, gain_two, shift_two))
    up_value = low_back(jnp.dot(normed2, w_up, precision=high) + bias_up)
    gelu_low = low(jax.nn.gelu(up_value, approximate=True))
    return middle + low_back(jnp.dot(gelu_low, w_down, precision=high) + bias_down)

def reference(hidden_in, segments, ln1_gain, ln1_shift, qkv_weight, query_bias, value_bias, dense_weight, dense_bias, ln2_gain, ln2_shift, up_weight, up_bias, down_weight, down_bias, out_grad):
    params = (hidden_in.astype(jnp.float32), ln1_gain.astype(jnp.float32), ln1_shift.astype(jnp.float32), qkv_weight.astype(jnp.float32), query_bias.astype(jnp.float32), value_bias.astype(jnp.float32), dense_weight.astype(jnp.float32), dense_bias.astype(jnp.float32), ln2_gain.astype(jnp.float32), ln2_shift.astype(jnp.float32), up_weight.astype(jnp.float32), up_bias.astype(jnp.float32), down_weight.astype(jnp.float32), down_bias.astype(jnp.float32))

    def closed(*inputs):
        return forward(*inputs, segments)
    block_out, pullback = jax.vjp(closed, *params)
    grads = pullback(out_grad.astype(jnp.float32))
    return (block_out, grads[0], grads[1], grads[2], grads[3], grads[4], grads[5], grads[6], grads[7], grads[8], grads[9], grads[10], grads[11], grads[12], grads[13])
```

```python
from functools import partial

import jax
import jax.numpy as jnp
from jax import lax
from jax.sharding import PartitionSpec as P

HEADS = 16
HEAD_DIM = 64
EPS = 1e-05
NEG = -1000000000.0
T = "tensor"
DP = "dp"
NT = 8
BLK = 80
PAD = NT * BLK
BF = jnp.bfloat16
F32 = jnp.float32


def norm_stats(values_in):
    row_mean = jnp.mean(values_in, -1, keepdims=True)
    centred = values_in - row_mean
    variance = jnp.mean(centred * centred, -1, keepdims=True)
    recip = lax.rsqrt(variance + EPS)
    return centred * recip, recip


def norm_backward(grad_out, normal_part, recip, gain_vec):
    scaled = grad_out * gain_vec
    return recip * (
        scaled
        - jnp.mean(scaled, -1, keepdims=True)
        - normal_part * jnp.mean(scaled * normal_part, -1, keepdims=True)
    )


def dot(a, b):
    return jnp.dot(a, b, preferred_element_type=F32)


def dot_nt(a, b):
    return lax.dot_general(a, b, (((1,), (1,)), ((), ())), preferred_element_type=F32)


def dot_tn(a, b):
    return lax.dot_general(a, b, (((0,), (0,)), ((), ())), preferred_element_type=F32)


def pad_rows(a):
    return jnp.pad(a, ((0, PAD - a.shape[0]), (0, 0)))


def block_of(a, j):
    return lax.dynamic_slice_in_dim(a, j * BLK, BLK, 0)


def gather_xor(piece):
    parts = [piece]
    for k in range(1, NT):
        parts.append(lax.ppermute(piece, T, [(i, i ^ k) for i in range(NT)]))
    return parts


def scatter_xor(parts):
    total = parts[0].astype(F32)
    got = [lax.ppermute(parts[k], T, [(i, i ^ k) for i in range(NT)]) for k in range(1, NT)]
    for piece in got:
        total = total + piece.astype(F32)
    return total


def natural(parts, me):
    stacked = jnp.stack(parts)
    return jnp.concatenate(
        [lax.dynamic_index_in_dim(stacked, me ^ j, 0, keepdims=False) for j in range(NT)], 0
    )


def exchange(a, axis, **more):
    return lax.all_to_all(a, axis, 0, 0, tiled=True, **more)


CORES = [(i, i ^ 1) for i in range(16)]
CHIPS = [[i for i in range(16) if i % 2 == c] for c in range(2)]


def reduce_rows(payload, core):
    half = payload.shape[0] // 2
    width = payload.shape[1]
    keep = lax.dynamic_slice_in_dim(payload, core * half, half, 0)
    give = lax.dynamic_slice_in_dim(payload, (1 - core) * half, half, 0).astype(BF)
    summed = (keep + lax.ppermute(give, DP, CORES).astype(F32)).astype(BF)
    got = exchange(summed.reshape(8, half // 8, width), DP, axis_index_groups=CHIPS)
    mine = jnp.sum(got.astype(F32), 0).astype(BF)
    full = exchange(
        jnp.broadcast_to(mine[None], (8,) + mine.shape), DP, axis_index_groups=CHIPS
    ).reshape(half, width)
    other = lax.ppermute(full, DP, CORES)
    first = jnp.where(core == 0, full, other)
    second = jnp.where(core == 0, other, full)
    return first, second


def per_device(
    hidden_in,
    segments,
    ln1_gain,
    ln1_shift,
    qkv_weight,
    query_bias,
    value_bias,
    dense_weight,
    dense_bias,
    ln2_gain,
    ln2_shift,
    up_weight,
    up_bias,
    down_weight,
    down_bias,
    out_grad,
):
    seq_len = hidden_in.shape[0]
    seg = segments[0]
    me = lax.axis_index(T)
    core = lax.axis_index(DP) % 2
    gelu_tanh = partial(jax.nn.gelu, approximate=True)
    scale = HEAD_DIM ** (-0.5)

    half_w = lax.dynamic_slice_in_dim(dense_weight, core * HEAD_DIM, HEAD_DIM, 0)
    own_w = exchange(jnp.broadcast_to(half_w[None], (NT,) + half_w.shape), T)
    other_w = lax.ppermute(own_w, DP, CORES)

    grad_low = out_grad.astype(BF)
    grad_pad = pad_rows(grad_low)
    grad_x = jnp.concatenate([block_of(grad_pad, me ^ k) for k in range(NT)], 0)
    hid_own = block_of(pad_rows(hidden_in), me)
    out_grad_own = block_of(pad_rows(out_grad), me)

    xhat1, recip1 = norm_stats(hidden_in)
    act_one = (xhat1 * ln1_gain + ln1_shift).astype(BF)
    zero_keys = jnp.zeros((2, HEAD_DIM), F32)
    qkv_bias = jnp.stack(
        [query_bias.reshape(2, HEAD_DIM), zero_keys, value_bias.reshape(2, HEAD_DIM)], axis=1
    ).reshape(-1)
    qkv_low = (dot(act_one, qkv_weight) + qkv_bias).astype(BF)
    pos = jnp.arange(seq_len)
    distance = (pos[None, :] - pos[:, None]).astype(F32)
    allowed = (distance <= 0) & (seg[:, None] == seg[None, :])
    slopes = jnp.exp2(-(8.0 / HEADS) * (me * 2 + jnp.arange(2) + 1).astype(F32))

    def part(h, c):
        start = (h * 3 + c) * HEAD_DIM
        return qkv_low[:, start : start + HEAD_DIM]

    def scores_of(h):
        raw = dot_nt(part(h, 0), part(h, 1)) * scale + slopes[h] * distance
        return jnp.where(allowed, raw, NEG)

    contexts, log_sums = [], []
    for h in range(2):
        s = scores_of(h)
        top = jnp.max(s, -1, keepdims=True)
        e = jnp.exp(s - top)
        total = jnp.sum(e, -1, keepdims=True)
        log_sums.append(top + jnp.log(total))
        contexts.append(dot((e / total).astype(BF), part(h, 2)).astype(BF))

    first = jnp.where(core == 0, contexts[0], contexts[1])
    second = jnp.where(core == 0, contexts[1], contexts[0])
    ctx_send = pad_rows(jnp.concatenate([first, second], 1)).reshape(NT, BLK, 2 * HEAD_DIM)
    ctx_got = exchange(ctx_send, T)
    ctx_a = jnp.transpose(ctx_got[:, :, :HEAD_DIM], (1, 0, 2)).reshape(BLK, NT * HEAD_DIM)
    ctx_b = jnp.transpose(ctx_got[:, :, HEAD_DIM:], (1, 0, 2)).reshape(BLK, NT * HEAD_DIM)
    attn = dot(ctx_a, own_w.reshape(NT * HEAD_DIM, -1)) + dot(
        ctx_b, other_w.reshape(NT * HEAD_DIM, -1)
    )
    attn = attn + dense_bias
    middle = hid_own + attn
    xhat2, recip2 = norm_stats(middle)
    act_two_own = (xhat2 * ln2_gain + ln2_shift).astype(BF)
    act_two = jnp.concatenate(gather_xor(act_two_own), 0)

    gelu_in_grad = dot_nt(grad_x, down_weight)
    up_value = dot(act_two, up_weight) + up_bias
    gelu_val, gelu_vjp = jax.vjp(gelu_tanh, up_value)
    gelu_low = gelu_val.astype(BF)
    up_low = gelu_vjp(gelu_in_grad)[0].astype(BF)
    norm_two_part = dot_nt(up_low, up_weight).astype(BF)
    norm_two_in = scatter_xor([norm_two_part[k * BLK : (k + 1) * BLK] for k in range(NT)])

    mlp_part = dot(gelu_low, down_weight).astype(BF)
    down_grad = dot_tn(gelu_low, grad_x)
    up_grad = dot_tn(act_two, up_low)
    up_bias_part = jnp.sum(up_low, 0, dtype=F32)
    down_bias_part = jnp.sum(grad_low, 0, dtype=F32)

    middle_grad = out_grad_own + norm_backward(norm_two_in, xhat2, recip2, ln2_gain)
    branch_own = middle_grad.astype(BF)
    branch = natural(gather_xor(branch_own), me)[:seq_len]
    ctx_grad = dot_nt(branch, dense_weight).astype(BF)

    mlp_own = scatter_xor([mlp_part[k * BLK : (k + 1) * BLK] for k in range(NT)])
    block_delta = (attn + mlp_own + down_bias).astype(BF)
    block_out = hidden_in + natural(gather_xor(block_delta), me)[:seq_len].astype(F32)

    early = jnp.concatenate(
        [jnp.concatenate([up_grad[:512], up_grad[512:]], 1), down_grad], 0
    )
    early_a, early_b = reduce_rows(early, core)
    up_weight_grad = jnp.concatenate([early_a[:, :512], early_a[:, 512:]], 0).astype(F32)
    down_weight_grad = early_b.astype(F32)

    grads = []
    for h in range(2):
        probs = jnp.exp(scores_of(h) - log_sums[h])
        cg = ctx_grad[:, h * HEAD_DIM : (h + 1) * HEAD_DIM]
        prob_grad = dot_nt(cg, part(h, 2))
        value_grad = dot_tn(probs.astype(BF), cg)
        score_low = (
            probs * (prob_grad - jnp.sum(prob_grad * probs, -1, keepdims=True))
        ).astype(BF)
        query_grad = dot(score_low, part(h, 1)) * scale
        key_grad = dot_tn(score_low, part(h, 0)) * scale
        grads += [query_grad, key_grad, value_grad]
    qkv_grad_low = jnp.concatenate(grads, 1).astype(BF)
    norm_one_part = dot_nt(qkv_grad_low, qkv_weight)
    gain_one_part = jnp.sum(norm_one_part * xhat1, 0)
    shift_one_part = jnp.sum(norm_one_part, 0)
    got = exchange(pad_rows(norm_one_part.astype(BF)).reshape(NT, BLK, -1), T)
    norm_one_in = jnp.sum(got.astype(F32), 0)
    xhat1_own, recip1_own = norm_stats(hid_own)
    in_delta = (
        middle_grad - out_grad_own + norm_backward(norm_one_in, xhat1_own, recip1_own, ln1_gain)
    ).astype(BF)
    input_grad = out_grad + natural(gather_xor(in_delta), me)[:seq_len].astype(F32)

    qkv_grad = dot_tn(act_one, qkv_grad_low)
    ctx_nat = jnp.concatenate(contexts, 1)
    dense_grad = dot_tn(ctx_nat, branch)
    late = jnp.concatenate(
        [
            qkv_grad[:512],
            qkv_grad[512:],
            jnp.concatenate([dense_grad[:, i * 256 : (i + 1) * 256] for i in range(4)], 0),
        ],
        1,
    )
    late_a, late_b = reduce_rows(late, core)
    late_full = jnp.concatenate([late_a, late_b], 0)
    qkv_weight_grad = jnp.concatenate([late_full[:, :384], late_full[:, 384:768]], 0).astype(F32)
    dense_weight_grad = jnp.concatenate(
        [late_full[i * 128 : (i + 1) * 128, 768:] for i in range(4)], 1
    ).astype(F32)

    part_sums = jnp.sum(qkv_grad_low, 0, dtype=F32)
    rows = [
        gain_one_part,
        shift_one_part,
        jnp.sum(norm_two_in * xhat2, 0),
        jnp.sum(norm_two_in, 0),
        jnp.sum(branch_own, 0, dtype=F32),
        down_bias_part,
        jnp.concatenate([up_bias_part, part_sums, jnp.zeros((128,), F32)]),
        jnp.zeros((1024,), F32),
    ]
    vecs = jnp.concatenate([r.reshape(8, 128) for r in rows], 0).reshape(16, 4, 128)
    mine = jnp.sum(exchange(vecs, DP), 0)
    summed = exchange(jnp.broadcast_to(mine[None], (16, 4, 128)), DP).reshape(64, 128)
    shared = summed[:40]
    for k in (1, 2, 4):
        shared = shared + lax.ppermute(shared, T, [(i, i ^ k) for i in range(NT)])
    shared = shared.reshape(5, 1024)
    last = summed[48:56].reshape(1024)
    sums = last[512:896].reshape(2, 3, HEAD_DIM)

    return (
        block_out,
        input_grad,
        shared[0],
        shared[1],
        qkv_weight_grad,
        sums[:, 0].reshape(-1),
        sums[:, 2].reshape(-1),
        dense_weight_grad,
        shared[4],
        shared[2],
        shared[3],
        up_weight_grad,
        last[:512],
        down_weight_grad,
        summed[40:48].reshape(1024),
    )


def solution(mesh):
    placed = (
        P("dp", None),
        P("dp", None),
        P(),
        P(),
        P(None, "tensor"),
        P("tensor"),
        P("tensor"),
        P("tensor", None),
        P(),
        P(),
        P(),
        P(None, "tensor"),
        P("tensor"),
        P("tensor", None),
        P(),
        P("dp", None),
    )
    return jax.shard_map(
        per_device,
        mesh=mesh,
        in_specs=placed,
        out_specs=(
            P("dp", None),
            P("dp", None),
            P(),
            P(),
            P(None, "tensor"),
            P("tensor"),
            P("tensor"),
            P("tensor", None),
            P(),
            P(),
            P(),
            P(None, "tensor"),
            P("tensor"),
            P("tensor", None),
            P(),
        ),
        check_vma=False,
    )
```

```python
from functools import partial

import jax
import jax.numpy as jnp
from jax import lax
from jax.experimental import pallas as pl
from jax.experimental.pallas import tpu as pltpu
from jax.sharding import PartitionSpec as P

HEADS = 16
HEAD_DIM = 64
EPS = 1e-05
NEG = -1000000000.0
T = "tensor"
DP = "dp"
NT = 8
BLK = 80
PAD = NT * BLK
BF = jnp.bfloat16
F32 = jnp.float32


def norm_stats(values_in):
    row_mean = jnp.mean(values_in, -1, keepdims=True)
    centred = values_in - row_mean
    variance = jnp.mean(centred * centred, -1, keepdims=True)
    recip = lax.rsqrt(variance + EPS)
    return centred * recip, recip


def norm_backward(grad_out, normal_part, recip, gain_vec):
    scaled = grad_out * gain_vec
    return recip * (
        scaled
        - jnp.mean(scaled, -1, keepdims=True)
        - normal_part * jnp.mean(scaled * normal_part, -1, keepdims=True)
    )


def dot(a, b):
    return jnp.dot(a, b, preferred_element_type=F32)


def dot_nt(a, b):
    return lax.dot_general(a, b, (((1,), (1,)), ((), ())), preferred_element_type=F32)


def dot_tn(a, b):
    return lax.dot_general(a, b, (((0,), (0,)), ((), ())), preferred_element_type=F32)


def pad_rows(a):
    return jnp.pad(a, ((0, PAD - a.shape[0]), (0, 0)))


def block_of(a, j):
    return lax.dynamic_slice_in_dim(a, j * BLK, BLK, 0)


def exchange(a, axis):
    return lax.all_to_all(a, axis, 0, 0, tiled=True)


def gather(piece):
    return exchange(jnp.broadcast_to(piece[None], (NT,) + piece.shape), T)


def hop(a, mask):
    return lax.ppermute(a, DP, [(i, i ^ mask) for i in range(16)])


def pick(a, j, axis=0):
    return lax.dynamic_index_in_dim(a, j, axis, keepdims=False)


def reduce_dp(payload, dp):
    core, y, z = dp % 2, (dp // 2) % 4, dp // 8
    rows, width = payload.shape
    chunk = rows // 16
    parts = payload.reshape(2, 2, 4, chunk, width)
    one = (pick(parts, core).astype(F32) + hop(pick(parts, 1 - core), 1).astype(F32)).astype(BF)
    two = pick(one, y, 1).astype(F32)
    for k in (1, 2, 3):
        two = two + hop(pick(one, y ^ k, 1), 2 * k).astype(F32)
    two = two.astype(BF)
    three = (pick(two, z).astype(F32) + hop(pick(two, 1 - z), 8).astype(F32)).astype(BF)
    by_z = jnp.stack([three, hop(three, 8)])
    by_y = jnp.stack([by_z] + [hop(by_z, 2 * k) for k in (1, 2, 3)])
    return jnp.stack([by_y, hop(by_y, 1)]).reshape(16, chunk, width)


def spread(perm_ref, got_ref, left_ref, right_ref):
    chunk = got_ref.shape[1]
    cut = left_ref.shape[1]
    for i in range(16):
        rows = got_ref[perm_ref[i]].astype(F32)
        left_ref[i * chunk : (i + 1) * chunk, :] = rows[:, :cut]
        right_ref[i * chunk : (i + 1) * chunk, :] = rows[:, cut:]


def natural_chunks(got, dp, cut):
    core, y, z = dp % 2, (dp // 2) % 4, dp // 8
    order = jnp.arange(16)
    c, zz, yy = order // 8, (order // 4) % 2, order % 4
    perm = ((c ^ core) * 8 + (yy ^ y) * 2 + (zz ^ z)).astype(jnp.int32)
    n, chunk, width = got.shape
    left, right = pl.pallas_call(
        spread,
        out_shape=[
            jax.ShapeDtypeStruct((n * chunk, cut), F32),
            jax.ShapeDtypeStruct((n * chunk, width - cut), F32),
        ],
        in_specs=[
            pl.BlockSpec(memory_space=pltpu.SMEM),
            pl.BlockSpec(memory_space=pltpu.VMEM),
        ],
        out_specs=[pl.BlockSpec(memory_space=pltpu.VMEM)] * 2,
        compiler_params=pltpu.CompilerParams(vmem_limit_bytes=32 << 20),
    )(perm, got)
    return left, right.T


def per_device(
    hidden_in,
    segments,
    ln1_gain,
    ln1_shift,
    qkv_weight,
    query_bias,
    value_bias,
    dense_weight,
    dense_bias,
    ln2_gain,
    ln2_shift,
    up_weight,
    up_bias,
    down_weight,
    down_bias,
    out_grad,
):
    seq_len = hidden_in.shape[0]
    seg = segments[0]
    me = lax.axis_index(T)
    dp = lax.axis_index(DP)
    core = dp % 2
    gelu_tanh = partial(jax.nn.gelu, approximate=True)
    scale = HEAD_DIM ** (-0.5)

    half_w = lax.dynamic_slice_in_dim(dense_weight, core * HEAD_DIM, HEAD_DIM, 0)
    own_w = gather(half_w)
    other_w = hop(own_w, 1)

    xhat1, recip1 = norm_stats(hidden_in)
    act_one = (xhat1 * ln1_gain + ln1_shift).astype(BF)
    zero_keys = jnp.zeros((2, HEAD_DIM), F32)
    qkv_bias = jnp.stack(
        [query_bias.reshape(2, HEAD_DIM), zero_keys, value_bias.reshape(2, HEAD_DIM)], axis=1
    ).reshape(-1)
    qkv_low = (dot(act_one, qkv_weight) + qkv_bias).astype(BF)
    pos = jnp.arange(seq_len)
    distance = (pos[None, :] - pos[:, None]).astype(F32)
    allowed = (distance <= 0) & (seg[:, None] == seg[None, :])
    slopes = jnp.exp2(-(8.0 / HEADS) * (me * 2 + jnp.arange(2) + 1).astype(F32))

    def part(h, c):
        start = (h * 3 + c) * HEAD_DIM
        return qkv_low[:, start : start + HEAD_DIM]

    def scores_of(h):
        raw = dot_nt(part(h, 0), part(h, 1)) * scale + slopes[h] * distance
        return jnp.where(allowed, raw, NEG)

    contexts, log_sums = [], []
    for h in range(2):
        s = scores_of(h)
        top = jnp.max(s, -1, keepdims=True)
        e = jnp.exp(s - top)
        total = jnp.sum(e, -1, keepdims=True)
        log_sums.append(top + jnp.log(total))
        contexts.append(dot((e / total).astype(BF), part(h, 2)).astype(BF))

    context = jnp.concatenate(contexts, 1)
    first = jnp.where(core == 0, contexts[0], contexts[1])
    second = jnp.where(core == 0, contexts[1], contexts[0])
    ctx_got = gather(pad_rows(jnp.concatenate([first, second], 1)))

    grad_low = out_grad.astype(BF)
    grad_pad = pad_rows(grad_low)
    gelu_in_grad = dot_nt(grad_pad, down_weight)
    hid_pad = pad_rows(hidden_in)

    ctx_a = jnp.concatenate([ctx_got[i, :, :HEAD_DIM] for i in range(NT)], 1)
    ctx_b = jnp.concatenate([ctx_got[i, :, HEAD_DIM:] for i in range(NT)], 1)
    attn = dot(ctx_a, own_w.reshape(NT * HEAD_DIM, -1)) + dot(
        ctx_b, other_w.reshape(NT * HEAD_DIM, -1)
    )
    middle = hid_pad + (attn + dense_bias)
    xhat2, recip2 = norm_stats(middle)
    act_two = (xhat2 * ln2_gain + ln2_shift).astype(BF)

    up_value = dot(act_two, up_weight) + up_bias
    gelu_val, gelu_vjp = jax.vjp(gelu_tanh, up_value)
    gelu_low = gelu_val.astype(BF)
    up_low = gelu_vjp(gelu_in_grad)[0].astype(BF)
    norm_two_part = dot_nt(up_low, up_weight).astype(BF)
    norm_two_in = jnp.sum(exchange(norm_two_part.reshape(NT, BLK, -1), T).astype(F32), 0)

    mlp_sum = lax.psum(dot(gelu_low[:seq_len], down_weight).astype(BF), T)
    up_bias_part = jnp.sum(up_low, 0, dtype=F32)
    down_bias_part = jnp.sum(grad_low, 0, dtype=F32)
    early = jnp.concatenate([dot_tn(act_two, up_low), dot_tn(grad_pad, gelu_low)], 1).astype(BF)
    early_got = reduce_dp(early, dp)
    up_weight_grad, down_weight_grad = natural_chunks(early_got, dp, 512)

    middle_own = block_of(middle, me)
    xhat2_own, recip2_own = norm_stats(middle_own)
    out_grad_own = block_of(pad_rows(out_grad), me)
    back_two = norm_backward(norm_two_in, xhat2_own, recip2_own, ln2_gain)
    branch_own = (out_grad_own + back_two).astype(BF)
    branch = gather(branch_own).reshape(PAD, -1)[:seq_len]
    ctx_grad = dot_nt(branch, dense_weight).astype(BF)

    grads = []
    for h in range(2):
        probs = jnp.exp(scores_of(h) - log_sums[h])
        cg = ctx_grad[:, h * HEAD_DIM : (h + 1) * HEAD_DIM]
        prob_grad = dot_nt(cg, part(h, 2))
        value_grad = dot_tn(probs.astype(BF), cg)
        score_low = (
            probs * (prob_grad - jnp.sum(prob_grad * probs, -1, keepdims=True))
        ).astype(BF)
        query_grad = dot(score_low, part(h, 1)) * scale
        key_grad = dot_tn(score_low, part(h, 0)) * scale
        grads += [query_grad, key_grad, value_grad]
    qkv_grad_low = jnp.concatenate(grads, 1).astype(BF)
    norm_one_part = dot_nt(qkv_grad_low, qkv_weight)
    gain_one_part = jnp.sum(norm_one_part * xhat1, 0)
    shift_one_part = jnp.sum(norm_one_part, 0)
    got = exchange(pad_rows(norm_one_part.astype(BF)).reshape(NT, BLK, -1), T)
    norm_one_in = jnp.sum(got.astype(F32), 0)
    hid_own = block_of(hid_pad, me)
    xhat1_own, recip1_own = norm_stats(hid_own)
    in_delta = (back_two + norm_backward(norm_one_in, xhat1_own, recip1_own, ln1_gain)).astype(BF)
    in_got, mlp_sum = lax.optimization_barrier((gather(in_delta), mlp_sum))
    input_grad = out_grad + in_got.reshape(PAD, -1)[:seq_len].astype(F32)
    block_out = middle[:seq_len] + (mlp_sum.astype(F32) + down_bias)

    late = jnp.concatenate([dot_tn(act_one, qkv_grad_low), dot_tn(branch, context)], 1).astype(BF)
    late_got = reduce_dp(late, dp)
    qkv_weight_grad, dense_weight_grad = natural_chunks(late_got, dp, 384)

    part_sums = jnp.sum(qkv_grad_low, 0, dtype=F32)
    rows = [
        gain_one_part,
        shift_one_part,
        jnp.sum(norm_two_in * xhat2_own, 0),
        jnp.sum(norm_two_in, 0),
        jnp.sum(branch_own, 0, dtype=F32),
        down_bias_part,
        jnp.concatenate([up_bias_part, part_sums, jnp.zeros((128,), F32)]),
        jnp.zeros((1024,), F32),
    ]
    summed = jnp.concatenate([r.reshape(8, 128) for r in rows], 0)
    for mask in (1, 2, 4, 8):
        summed = summed + hop(summed, mask)
    shared = summed[:40]
    for k in (1, 2, 4):
        shared = shared + lax.ppermute(shared, T, [(i, i ^ k) for i in range(NT)])
    shared = shared.reshape(5, 1024)
    last = summed[48:56].reshape(1024)
    sums = last[512:896].reshape(2, 3, HEAD_DIM)

    return (
        block_out,
        input_grad,
        shared[0],
        shared[1],
        qkv_weight_grad,
        sums[:, 0].reshape(-1),
        sums[:, 2].reshape(-1),
        dense_weight_grad,
        shared[4],
        shared[2],
        shared[3],
        up_weight_grad,
        last[:512],
        down_weight_grad,
        summed[40:48].reshape(1024),
    )


def solution(mesh):
    placed = (
        P("dp", None),
        P("dp", None),
        P(),
        P(),
        P(None, "tensor"),
        P("tensor"),
        P("tensor"),
        P("tensor", None),
        P(),
        P(),
        P(),
        P(None, "tensor"),
        P("tensor"),
        P("tensor", None),
        P(),
        P("dp", None),
    )
    return jax.shard_map(
        per_device,
        mesh=mesh,
        in_specs=placed,
        out_specs=(
            P("dp", None),
            P("dp", None),
            P(),
            P(),
            P(None, "tensor"),
            P("tensor"),
            P("tensor"),
            P("tensor", None),
            P(),
            P(),
            P(),
            P(None, "tensor"),
            P("tensor"),
            P("tensor", None),
            P(),
        ),
        check_vma=False,
    )
```

```python
from functools import partial

import jax
import jax.numpy as jnp
from jax import lax
from jax.experimental import pallas as pl
from jax.experimental.pallas import tpu as pltpu
from jax.sharding import PartitionSpec as P

HEADS = 16
HEAD_DIM = 64
EPS = 1e-05
NEG = -1000000000.0
T = "tensor"
DP = "dp"
NT = 8
BLK = 80
PAD = NT * BLK
BF = jnp.bfloat16
F32 = jnp.float32


def norm_stats(values_in):
    row_mean = jnp.mean(values_in, -1, keepdims=True)
    centred = values_in - row_mean
    variance = jnp.mean(centred * centred, -1, keepdims=True)
    recip = lax.rsqrt(variance + EPS)
    return centred * recip, recip


def norm_backward(grad_out, normal_part, recip, gain_vec):
    scaled = grad_out * gain_vec
    return recip * (
        scaled
        - jnp.mean(scaled, -1, keepdims=True)
        - normal_part * jnp.mean(scaled * normal_part, -1, keepdims=True)
    )


def dot(a, b):
    return jnp.dot(a, b, preferred_element_type=F32)


def dot_nt(a, b):
    return lax.dot_general(a, b, (((1,), (1,)), ((), ())), preferred_element_type=F32)


def dot_tn(a, b):
    return lax.dot_general(a, b, (((0,), (0,)), ((), ())), preferred_element_type=F32)


def pad_rows(a):
    return jnp.pad(a, ((0, PAD - a.shape[0]), (0, 0)))


def block_of(a, j):
    return lax.dynamic_slice_in_dim(a, j * BLK, BLK, 0)


def exchange(a, axis):
    return lax.all_to_all(a, axis, 0, 0, tiled=True)


def gather(piece):
    return exchange(jnp.broadcast_to(piece[None], (NT,) + piece.shape), T)


def hop(a, mask):
    return lax.ppermute(a, DP, [(i, i ^ mask) for i in range(16)])


def tensor_hop(a, mask):
    return lax.ppermute(a, T, [(i, i ^ mask) for i in range(NT)])


def pick(a, j, axis=0):
    return lax.dynamic_index_in_dim(a, j, axis, keepdims=False)


def place(dp):
    return dp % 2, (dp // 2) % 4, dp // 8


def z_add(two, got):
    return (two.astype(F32) + got.astype(F32)).astype(BF)


def y_spread(by_z):
    return tuple(hop(by_z, 2 * k) for k in (1, 2, 3))


def spread(where_ref, own_ref, other_ref, left_ref, right_ref):
    chunk = own_ref.shape[2]
    cut = left_ref.shape[1]
    core, y = where_ref[0], where_ref[1]
    for c in range(2):
        for z in range(2):
            for pair in (0, 2):
                parts = []
                for j in (pair, pair + 1):
                    a, b = own_ref[y ^ j, z], other_ref[y ^ j, z]
                    parts.append(jnp.where(core == c, a.astype(F32), b.astype(F32)))
                rows = jnp.concatenate(parts, 0)
                lo = (c * 8 + z * 4 + pair) * chunk
                left_ref[lo : lo + 2 * chunk, :] = rows[:, :cut]
                right_ref[:, lo : lo + 2 * chunk] = jnp.transpose(rows[:, cut:])


def natural_chunks(own, other, dp, cut):
    core, y, _ = place(dp)
    n, chunk, width = 16, own.shape[2], own.shape[3]
    return pl.pallas_call(
        spread,
        out_shape=[shaped(n * chunk, cut), shaped(width - cut, n * chunk)],
        in_specs=[SMEM_SPEC] + whole(2),
        out_specs=whole(2),
        compiler_params=BIG,
        cost_estimate=SHORT,
    )(jnp.stack([core, y]).astype(jnp.int32), *far(own, other))


def attend_forward(
    where_ref, hid_ref, gain_ref, shift_ref, w_ref, qb_ref, vb_ref, srow_ref, scol_ref,
    act_ref, qkv_ref, ctx_ref, send_ref, lse_ref,
):
    seq_len = hid_ref.shape[0]
    for lo, hi in row_blocks(seq_len):
        xhat, _ = norm_stats(hid_ref[lo:hi, :])
        act_ref[lo:hi, :] = (xhat * gain_ref[...] + shift_ref[...]).astype(BF)
    none = jnp.zeros((1, HEAD_DIM), F32)
    cut = HEAD_DIM
    bias = jnp.concatenate(
        [qb_ref[:, :cut], none, vb_ref[:, :cut], qb_ref[:, cut:], none, vb_ref[:, cut:]], 1
    )
    for lo, hi in halves(seq_len):
        qkv_ref[lo:hi, :] = (dot(act_ref[lo:hi, :], w_ref[...]) + bias).astype(BF)
    even = where_ref[1] == 0
    slopes = head_slopes(where_ref)
    for lo, hi in row_blocks(seq_len):
        allowed, distance = masks(lo, hi, srow_ref, scol_ref)
        outs = []
        for h in range(2):
            s = head_scores(qkv_ref, slopes, h, lo, hi, allowed, distance)
            top = jnp.max(s, -1, keepdims=True)
            e = jnp.exp(s - top)
            total = jnp.sum(e, -1, keepdims=True)
            lse_ref[h, lo:hi, :] = top + jnp.log(total)
            p = (e / total).astype(BF)
            outs.append(dot(p, qkv_ref[:hi, head_part(h, 2)]).astype(BF))
        ctx_ref[lo:hi, :] = jnp.concatenate(outs, 1)
        first = jnp.where(even, outs[0].astype(F32), outs[1].astype(F32))
        second = jnp.where(even, outs[1].astype(F32), outs[0].astype(F32))
        both = jnp.concatenate([first, second], 1).astype(BF)
        for i in range(NT):
            send_ref[i, lo:hi, :] = both
    pad = jnp.zeros((PAD - seq_len, 2 * HEAD_DIM), BF)
    for i in range(NT):
        send_ref[i, seq_len:, :] = pad


def row_blocks(n):
    return [(lo, min(lo + 128, n)) for lo in range(0, n, 128)]


def halves(n):
    return [(0, 304), (304, n)]


def head_part(h, c):
    start = (h * 3 + c) * HEAD_DIM
    return slice(start, start + HEAD_DIM)


def head_slopes(where_ref):
    first = (where_ref[0] * 2).astype(F32)
    return [
        jnp.exp2(jnp.full((1, 1), -(8.0 / HEADS), F32) * (first + (h + 1.0))) for h in range(2)
    ]


def masks(lo, hi, srow_ref, scol_ref):
    shape = (hi - lo, hi)
    diff = lax.broadcasted_iota(jnp.int32, shape, 1) - lax.broadcasted_iota(jnp.int32, shape, 0) - lo
    allowed = (diff <= 0) & (scol_ref[lo:hi, :] == srow_ref[:, :hi])
    return allowed, diff.astype(F32)


def head_scores(qkv_ref, slopes, h, lo, hi, allowed, distance):
    raw = dot_nt(qkv_ref[lo:hi, head_part(h, 0)], qkv_ref[:hi, head_part(h, 1)])
    return jnp.where(allowed, raw * HEAD_DIM ** (-0.5) + slopes[h] * distance, NEG)


def attend_backward(
    where_ref, branch_ref, wd_ref, qkv_ref, lse_ref, srow_ref, scol_ref, w_ref,
    grad_ref, part_ref, acc_ref, cg_ref,
):
    seq_len = qkv_ref.shape[0]
    scale = HEAD_DIM ** (-0.5)
    for i in (0, 4):
        rows = jnp.concatenate([branch_ref[j, :BLK, :] for j in range(i, i + 4)], 0)
        cg_ref[i * BLK : (i + 4) * BLK, :] = dot_nt(rows, wd_ref[...]).astype(BF)
    total = branch_ref[0, BLK:, :].astype(F32)
    for j in range(1, NT):
        total = total + branch_ref[j, BLK:, :].astype(F32)
    total = total.astype(BF)
    for j in range(NT):
        part_ref[j, BLK:, :] = total
    acc_ref[...] = jnp.zeros_like(acc_ref)
    slopes = head_slopes(where_ref)
    for lo, hi in row_blocks(seq_len):
        allowed, distance = masks(lo, hi, srow_ref, scol_ref)
        cg_all = cg_ref[lo:hi, :]
        for h in range(2):
            s = head_scores(qkv_ref, slopes, h, lo, hi, allowed, distance)
            p = jnp.exp(s - lse_ref[h, lo:hi, :])
            cg = cg_all[:, h * HEAD_DIM : (h + 1) * HEAD_DIM]
            pg = dot_nt(cg, qkv_ref[:hi, head_part(h, 2)])
            acc_ref[2 * h + 1, :, :hi] += dot_tn(cg, p.astype(BF))
            sg = (p * (pg - jnp.sum(pg * p, -1, keepdims=True))).astype(BF)
            grad_ref[lo:hi, head_part(h, 0)] = (
                dot(sg, qkv_ref[:hi, head_part(h, 1)]) * scale
            ).astype(BF)
            acc_ref[2 * h, :, :hi] += dot_tn(qkv_ref[lo:hi, head_part(h, 0)], sg)
    for h in range(2):
        kg = jnp.transpose(acc_ref[2 * h, :, :]) * scale
        vg = jnp.transpose(acc_ref[2 * h + 1, :, :])
        grad_ref[:, head_part(h, 1)] = kg.astype(BF)
        grad_ref[:, head_part(h, 2)] = vg.astype(BF)
    for h in range(2):
        grad_ref[seq_len:, head_part(h, 0)] = jnp.zeros((PAD - seq_len, HEAD_DIM), BF)
    for lo in range(0, PAD, 320):
        part = dot_nt(grad_ref[lo : lo + 320, :], w_ref[...]).astype(BF)
        for j in range(4):
            part_ref[lo // BLK + j, :BLK, :] = part[j * BLK : (j + 1) * BLK, :]


def feed(
    ctx_ref, own_ref, other_ref, hid_ref, db_ref, gain_ref, shift_ref, up_ref, ub_ref, gin_ref,
    mid_ref, act_ref, gelu_ref, low_ref, part_ref, sum_ref,
):
    step = pl.program_id(0)
    ctx_a = jnp.concatenate([ctx_ref[i, :, :HEAD_DIM] for i in range(NT)], 1)
    ctx_b = jnp.concatenate([ctx_ref[i, :, HEAD_DIM:] for i in range(NT)], 1)
    attn = dot(ctx_a, own_ref[...]) + dot(ctx_b, other_ref[...])
    middle = hid_ref[...] + (attn + db_ref[...])
    mid_ref[...] = middle
    xhat, _ = norm_stats(middle)
    act = (xhat * gain_ref[...] + shift_ref[...]).astype(BF)
    act_ref[...] = act
    x = dot(act, up_ref[...]) + ub_ref[...]
    a = 0.7978845608028654
    t = jnp.tanh(a * (x + 0.044715 * x * x * x))
    gelu_ref[...] = (x * (0.5 * (1.0 + t))).astype(BF)
    slope = 0.5 * (1.0 + t) + 0.5 * x * (1.0 - t * t) * (a * (1.0 + 3 * 0.044715 * x * x))
    low = (gin_ref[...] * slope).astype(BF)
    low_ref[...] = low
    part_ref[...] = dot_nt(low, up_ref[...]).astype(BF)

    @pl.when(step == 0)
    def _():
        sum_ref[...] = jnp.zeros_like(sum_ref)

    sum_ref[...] += jnp.sum(low.astype(F32), 0, keepdims=True)


def norm_two_back(
    me_ref, got_ref, mid_ref, og_ref, gain_ref, mlp_ref, back_ref, send_ref, sum_ref
):
    total = got_ref[0].astype(F32)
    for i in range(1, NT):
        total = total + got_ref[i].astype(F32)
    xhat, recip = norm_stats(mid_ref[...])
    back = norm_backward(total, xhat, recip, gain_ref[...])
    back_ref[...] = back
    branch = (og_ref[...] + back).astype(BF)
    for i in range(NT):
        send_ref[i, :BLK, :] = branch
        send_ref[i, BLK:, :] = mlp_ref[i]
    sum_ref[0:1, :] = jnp.sum(total * xhat, 0, keepdims=True)
    sum_ref[1:2, :] = jnp.sum(total, 0, keepdims=True)
    sum_ref[2:3, :] = jnp.sum(branch.astype(F32), 0, keepdims=True)
    sum_ref[3:8, :] = jnp.zeros((5, sum_ref.shape[1]), F32)


def norm_one_back(me_ref, got_ref, hid_ref, back_ref, gain_ref, vec_ref, send_ref):
    total = got_ref[0].astype(F32)
    for i in range(1, NT):
        total = total + got_ref[i].astype(F32)
    xhat, recip = norm_stats(hid_ref[...])
    delta = (back_ref[...] + norm_backward(total, xhat, recip, gain_ref[...])).astype(BF)
    pairs = [vec_ref[2 * i : 2 * i + 2, :] for i in range(8)]
    vec = jnp.concatenate([jnp.concatenate([p[:1], p[1:]], 1) for p in pairs], 0)
    both = jnp.concatenate(split(vec), 0)
    for i in range(NT):
        send_ref[i, :BLK, :] = delta
        send_ref[i, BLK:, :] = both


def mlp_out(gelu_ref, w_ref, out_ref):
    for lo in (0, 320):
        out_ref[lo : lo + 320, :] = dot(gelu_ref[lo : lo + 320, :], w_ref[...]).astype(BF)


def early_grads(where_ref, act_ref, low_ref, grad_ref, gelu_ref, keep_ref, give_ref, sum_ref):
    half = keep_ref.shape[0]
    for ref, side in ((keep_ref, where_ref[1]), (give_ref, 1 - where_ref[1])):
        cols = pl.ds(pl.multiple_of(side * half, half), half)
        ref[:, :512] = dot_tn(act_ref[:, cols], low_ref[...]).astype(BF)
        ref[:, 512:] = dot_tn(grad_ref[:, cols], gelu_ref[...]).astype(BF)
    sum_ref[...] = jnp.sum(grad_ref[...].astype(F32), 0, keepdims=True)


def split(v):
    high = v.astype(BF)
    return high, (v - high.astype(F32)).astype(BF)


def join(high, low):
    return high.astype(F32) + low.astype(F32)


def late_grads(
    where_ref, act_ref, grad_ref, branch_ref, ctx_ref, part_ref, hid_ref, two_ref, up_ref,
    down_ref, keep_ref, give_ref, vec_ref,
):
    seq_len, width = act_ref.shape
    half = width // 2
    for ref, side in ((keep_ref, where_ref[1]), (give_ref, 1 - where_ref[1])):
        cols = pl.ds(pl.multiple_of(side * half, half), half)
        ref[:half, :384] = dot_tn(act_ref[:, cols], grad_ref[:seq_len, :]).astype(BF)
        branch = jnp.concatenate([branch_ref[j, :BLK, cols] for j in range(NT)], 0)
        ref[:half, 384:] = dot_tn(branch[:seq_len], ctx_ref[...]).astype(BF)
    gain = jnp.zeros((1, width), F32)
    shift = gain
    for j in range(NT):
        lo, hi = j * BLK, min(j * BLK + BLK, seq_len)
        xhat, _ = norm_stats(hid_ref[lo:hi, :])
        part = part_ref[j, : hi - lo, :].astype(F32)
        gain = gain + jnp.sum(part * xhat, 0, keepdims=True)
        shift = shift + jnp.sum(part, 0, keepdims=True)
    sums = jnp.sum(grad_ref[...].astype(F32), 0, keepdims=True)
    last = jnp.concatenate([up_ref[...], sums, jnp.zeros((1, 128), F32)], 1)
    vectors = [
        gain, shift, two_ref[0:1, :], two_ref[1:2, :], two_ref[2:3, :], down_ref[...], last,
        jnp.zeros_like(last),
    ]
    for i, v in enumerate(vectors):
        vec_ref[2 * i : 2 * i + 1, :] = v[:, :half]
        vec_ref[2 * i + 1 : 2 * i + 2, :] = v[:, half:]
    high, low = split(vec_ref[...])
    give_ref[half : half + 16, :] = high
    give_ref[half + 16 :, :] = low


def early_core(where_ref, keep_ref, got_ref, own_ref, one_ref, two_ref, three_ref):
    y = where_ref[2]
    for k, ref in enumerate((own_ref, one_ref, two_ref, three_ref)):
        for z in range(2):
            total = keep_ref[z, y ^ k].astype(F32) + got_ref[z, y ^ k].astype(F32)
            ref[z] = total.astype(BF)


def late_core(
    where_ref, keep_ref, got_ref, vec_ref, own_ref, one_ref, two_ref, three_ref, out_ref
):
    y = where_ref[2]
    chunk = keep_ref.shape[2]
    half = 8 * chunk
    vec = vec_ref[...] + join(got_ref[half : half + 16, :], got_ref[half + 16 :, :])
    out_ref[...] = vec
    parts = split(vec)
    for k, ref in enumerate((own_ref, one_ref, two_ref, three_ref)):
        for z in range(2):
            rows = pl.ds(pl.multiple_of((z * 4 + (y ^ k)) * chunk, chunk), chunk)
            total = keep_ref[z, y ^ k].astype(F32) + got_ref[rows, :].astype(F32)
            ref[z, :chunk, :] = total.astype(BF)
            ref[z, chunk:, :] = parts[z]


def late_y(own_ref, one_ref, two_ref, three_ref, vec_ref, out_ref, sum_ref):
    chunk = own_ref.shape[1] - 16
    vec = vec_ref[...]
    for ref in (one_ref, two_ref, three_ref):
        vec = vec + join(ref[0, chunk:, :], ref[1, chunk:, :])
    sum_ref[...] = vec
    parts = split(vec)
    for z in range(2):
        total = own_ref[z, :chunk, :].astype(F32)
        for ref in (one_ref, two_ref, three_ref):
            total = total + ref[z, :chunk, :].astype(F32)
        out_ref[z, :chunk, :] = total.astype(BF)
        out_ref[z, chunk:, :] = parts[z]


def late_z(own_ref, got_ref, vec_ref, out_ref, sum_ref):
    chunk = out_ref.shape[1]
    sum_ref[...] = vec_ref[...] + join(got_ref[0, chunk:, :], got_ref[1, chunk:, :])
    for z in range(2):
        total = own_ref[z, :chunk, :].astype(F32) + got_ref[z, :chunk, :].astype(F32)
        out_ref[z] = total.astype(BF)


def add_rows(mid_ref, got_ref, bias_ref, out_ref):
    out_ref[...] = mid_ref[...] + (got_ref[0].astype(F32) + bias_ref[...])


def simple(kernel, outs, *args):
    return pl.pallas_call(
        kernel,
        out_shape=outs,
        in_specs=whole(len(args)),
        out_specs=whole(len(outs)),
        compiler_params=BIG,
        cost_estimate=TINY,
    )(*far(*args))


def simple_at(kernel, outs, where, *args, cost=None):
    return pl.pallas_call(
        kernel,
        out_shape=outs,
        in_specs=[SMEM_SPEC] + whole(len(args)),
        out_specs=whole(len(outs)),
        compiler_params=BIG,
        cost_estimate=cost or TINY,
    )(where, *far(*args))


def whole(n):
    return [pl.BlockSpec(memory_space=pltpu.VMEM)] * n


SMEM_SPEC = pl.BlockSpec(memory_space=pltpu.SMEM)
LONG = pl.CostEstimate(flops=4 << 30, bytes_accessed=24 << 20, transcendentals=0)
SHORT = pl.CostEstimate(flops=1 << 20, bytes_accessed=10 << 20, transcendentals=0)
TINY = pl.CostEstimate(flops=1, bytes_accessed=1, transcendentals=0)
BIG = pltpu.CompilerParams(vmem_limit_bytes=40 << 20)


def shaped(*shape, dtype=F32):
    return pltpu.HBM(shape, dtype)


def far(*arrays):
    return [pltpu.with_memory_space_constraint(a, pltpu.HBM) for a in arrays]


def tie(*arrays):
    return lax.optimization_barrier(arrays)


def per_device(
    hidden_in,
    segments,
    ln1_gain,
    ln1_shift,
    qkv_weight,
    query_bias,
    value_bias,
    dense_weight,
    dense_bias,
    ln2_gain,
    ln2_shift,
    up_weight,
    up_bias,
    down_weight,
    down_bias,
    out_grad,
):
    seq_len, width = hidden_in.shape
    me = lax.axis_index(T)
    dp = lax.axis_index(DP)
    core = dp % 2
    row = lambda v: v.reshape(1, -1)
    where = jnp.stack([me, core, (dp // 2) % 4]).astype(jnp.int32)

    half_w = lax.dynamic_slice_in_dim(dense_weight, core * HEAD_DIM, HEAD_DIM, 0)
    own_w = gather(half_w).reshape(NT * HEAD_DIM, width)
    other_w = hop(own_w, 1)

    seg_col = segments.reshape(seq_len, 1)
    act_one, qkv_low, context, ctx_send, lse = pl.pallas_call(
        attend_forward,
        out_shape=[
            shaped(seq_len, width, dtype=BF),
            shaped(seq_len, 384, dtype=BF),
            shaped(seq_len, 128, dtype=BF),
            shaped(NT, PAD, 128, dtype=BF),
            shaped(2, seq_len, 1),
        ],
        in_specs=[SMEM_SPEC] + whole(8),
        out_specs=whole(5),
        compiler_params=BIG,
        cost_estimate=LONG,
    )(
        where,
        *far(hidden_in),
        row(ln1_gain),
        row(ln1_shift),
        *far(qkv_weight),
        row(query_bias),
        row(value_bias),
        segments,
        seg_col,
    )
    ctx_got = exchange(ctx_send, T)

    grad_pad = pad_rows(out_grad.astype(BF))
    gelu_in_grad = dot_nt(grad_pad, down_weight)
    hid_pad = pad_rows(hidden_in)
    out_grad_pad = pad_rows(out_grad)

    rows = 320
    tile = lambda w: pl.BlockSpec((rows, w), lambda i: (i, 0))
    fixed = lambda *shape: pl.BlockSpec(shape, lambda i: (0,) * len(shape))
    middle, act_two, gelu_low, up_low, norm_two_part, up_bias_part = pl.pallas_call(
        feed,
        grid=(PAD // rows,),
        out_shape=[
            shaped(PAD, width),
            shaped(PAD, width, dtype=BF),
            shaped(PAD, 512, dtype=BF),
            shaped(PAD, 512, dtype=BF),
            shaped(PAD, width, dtype=BF),
            shaped(1, 512),
        ],
        in_specs=[
            pl.BlockSpec((NT, rows, 128), lambda i: (0, i, 0)),
            fixed(512, width),
            fixed(512, width),
            tile(width),
            fixed(1, width),
            fixed(1, width),
            fixed(1, width),
            fixed(width, 512),
            fixed(1, 512),
            tile(512),
        ],
        out_specs=[tile(width), tile(width), tile(512), tile(512), tile(width), fixed(1, 512)],
        compiler_params=BIG,
        cost_estimate=TINY,
    )(
        *far(ctx_got, own_w, other_w, hid_pad),
        row(dense_bias),
        row(ln2_gain),
        row(ln2_shift),
        *far(up_weight),
        row(up_bias),
        *far(gelu_in_grad),
    )
    two_got = exchange(norm_two_part.reshape(NT, BLK, width), T)

    mlp_part = pl.pallas_call(
        mlp_out,
        out_shape=shaped(PAD, width, dtype=BF),
        in_specs=whole(2),
        out_specs=whole(1)[0],
        compiler_params=BIG,
        cost_estimate=TINY,
    )(*far(gelu_low, down_weight))
    e_keep, e_give, down_bias_part = simple_at(
        early_grads,
        [shaped(512, width, dtype=BF), shaped(512, width, dtype=BF), shaped(1, width)],
        where, act_two, up_low, grad_pad, gelu_low,
    )
    e_core = hop(e_give, 1)
    two_got, e_core, mlp_part = tie(two_got, e_core, mlp_part)

    mine = pl.BlockSpec((BLK, width), lambda i, m: (m[0], 0))
    zero = lambda *shape: pl.BlockSpec(shape, lambda i, m: (0,) * len(shape))
    back_two, branch_send, sums_two = pl.pallas_call(
        norm_two_back,
        out_shape=[shaped(BLK, width), shaped(NT, 2 * BLK, width, dtype=BF), shaped(8, width)],
        grid_spec=pltpu.PrefetchScalarGridSpec(
            num_scalar_prefetch=1,
            grid=(1,),
            in_specs=[
                zero(NT, BLK, width), mine, mine, zero(1, width), zero(NT, BLK, width)
            ],
            out_specs=[zero(BLK, width), zero(NT, 2 * BLK, width), zero(8, width)],
        ),
        compiler_params=BIG,
        cost_estimate=TINY,
    )(
        me.reshape(1),
        *far(two_got, middle, out_grad_pad),
        row(ln2_gain),
        *far(mlp_part.reshape(NT, BLK, width)),
    )
    branch = exchange(branch_send, T)

    e_core, branch_send = tie(e_core, branch_send)
    e_own, *e_y = simple_at(
        early_core,
        [shaped(2, 64, width, dtype=BF)] * 4,
        where, e_keep.reshape(2, 4, 64, width), e_core.reshape(2, 4, 64, width),
    )
    e_y = tie(*[hop(e, 2 * (k + 1)) for k, e in enumerate(e_y)])
    e_two = sum([e.astype(F32) for e in e_y], e_own.astype(F32)).astype(BF)
    branch, e_two = tie(branch, e_two)
    e_z = hop(e_two, 8)

    qkv_grad_low, norm_one_part = pl.pallas_call(
        attend_backward,
        out_shape=[shaped(PAD, 384, dtype=BF), shaped(NT, 2 * BLK, width, dtype=BF)],
        in_specs=[SMEM_SPEC] + whole(7),
        out_specs=whole(2),
        scratch_shapes=[pltpu.VMEM((4, HEAD_DIM, PAD), F32), pltpu.VMEM((PAD, 128), BF)],
        compiler_params=BIG,
        cost_estimate=LONG,
    )(where, *far(branch, dense_weight, qkv_low, lse), segments, seg_col, *far(qkv_weight))
    norm_one_part, e_z = tie(norm_one_part, e_z)
    one_got = exchange(norm_one_part, T)

    e_three = z_add(e_two, e_z)
    e_y = y_spread(e_three)
    l_keep, l_give, vec = simple_at(
        late_grads,
        [shaped(512, 512, dtype=BF), shaped(544, 512, dtype=BF), shaped(16, 512)],
        where, act_one, qkv_grad_low, branch, context, norm_one_part, hidden_in, sums_two,
        up_bias_part, down_bias_part, cost=LONG,
    )
    l_core, *e_y = tie(hop(l_give, 1), *e_y)
    l_own, *l_y, vec = simple_at(
        late_core,
        [shaped(2, 80, 512, dtype=BF)] * 4 + [shaped(16, 512)],
        where, l_keep.reshape(2, 4, 64, 512), l_core, vec,
    )
    e_by_y = jnp.stack([e_three, *e_y])
    e_core, *l_y = tie(hop(e_by_y, 1), *[hop(p, 2 * (k + 1)) for k, p in enumerate(l_y)])
    l_two, vec = simple(
        late_y, [shaped(2, 80, 512, dtype=BF), shaped(16, 512)], l_own, *l_y, vec
    )
    one_got, l_two, vec, e_core, e_by_y = tie(one_got, l_two, vec, e_core, e_by_y)
    l_three, vec = simple(
        late_z, [shaped(2, 64, 512, dtype=BF), shaped(16, 512)], l_two, hop(l_two, 8), vec
    )

    in_send = pl.pallas_call(
        norm_one_back,
        out_shape=shaped(NT, BLK + 16, width, dtype=BF),
        grid_spec=pltpu.PrefetchScalarGridSpec(
            num_scalar_prefetch=1,
            grid=(1,),
            in_specs=[
                zero(NT, BLK, width), mine, zero(BLK, width), zero(1, width), zero(16, 512)
            ],
            out_specs=zero(NT, BLK + 16, width),
        ),
        compiler_params=BIG,
        cost_estimate=TINY,
    )(me.reshape(1), *far(one_got, hid_pad, back_two), row(ln1_gain), *far(vec))
    in_send, l_three, one_got, e_core, e_by_y = tie(in_send, l_three, one_got, e_core, e_by_y)
    in_got = exchange(in_send, T)

    l_by_y = jnp.stack([l_three, *y_spread(l_three)])
    up_weight_grad, down_weight_grad = natural_chunks(e_by_y, e_core, dp, 512)
    block_out = pl.pallas_call(
        add_rows,
        grid=(NT,),
        out_shape=shaped(seq_len, width),
        in_specs=[
            pl.BlockSpec((BLK, width), lambda i: (i, 0)),
            pl.BlockSpec((1, BLK, width), lambda i: (i, 1, 0)),
            fixed(1, width),
        ],
        out_specs=pl.BlockSpec((BLK, width), lambda i: (i, 0)),
        compiler_params=BIG,
        cost_estimate=SHORT,
    )(*far(middle, one_got), row(down_bias))
    in_got, l_by_y, up_weight_grad, down_weight_grad, block_out = tie(
        in_got, l_by_y, up_weight_grad, down_weight_grad, block_out
    )
    l_core = hop(l_by_y, 1)
    shared = jnp.sum(in_got[:, BLK : BLK + 8].astype(F32) + in_got[:, BLK + 8 :].astype(F32), 0)
    summed = vec.reshape(8, 1024)
    input_grad = out_grad + in_got[:, :BLK].reshape(PAD, width)[:seq_len].astype(F32)
    qkv_weight_grad, dense_weight_grad = natural_chunks(l_by_y, l_core, dp, 384)
    last = summed[6]
    sums = last[512:896].reshape(2, 3, HEAD_DIM)

    return (
        block_out,
        input_grad,
        shared[0],
        shared[1],
        qkv_weight_grad,
        sums[:, 0].reshape(-1),
        sums[:, 2].reshape(-1),
        dense_weight_grad,
        shared[4],
        shared[2],
        shared[3],
        up_weight_grad,
        last[:512],
        down_weight_grad,
        summed[5],
    )


def solution(mesh):
    placed = (
        P("dp", None),
        P("dp", None),
        P(),
        P(),
        P(None, "tensor"),
        P("tensor"),
        P("tensor"),
        P("tensor", None),
        P(),
        P(),
        P(),
        P(None, "tensor"),
        P("tensor"),
        P("tensor", None),
        P(),
        P("dp", None),
    )
    return jax.shard_map(
        per_device,
        mesh=mesh,
        in_specs=placed,
        out_specs=(
            P("dp", None),
            P("dp", None),
            P(),
            P(),
            P(None, "tensor"),
            P("tensor"),
            P("tensor"),
            P("tensor", None),
            P(),
            P(),
            P(),
            P(None, "tensor"),
            P("tensor"),
            P("tensor", None),
            P(),
        ),
        check_vma=False,
    )
```

```python
from functools import partial

import jax
import jax.numpy as jnp
from jax import lax
from jax.experimental import pallas as pl
from jax.experimental.pallas import tpu as pltpu
from jax.sharding import PartitionSpec as P

HEADS = 16
HEAD_DIM = 64
EPS = 1e-05
NEG = -1000000000.0
T = "tensor"
DP = "dp"
NT = 8
BLK = 80
PAD = NT * BLK
BF = jnp.bfloat16
F32 = jnp.float32


def norm_stats(values_in):
    row_mean = jnp.mean(values_in, -1, keepdims=True)
    centred = values_in - row_mean
    variance = jnp.mean(centred * centred, -1, keepdims=True)
    recip = lax.rsqrt(variance + EPS)
    return centred * recip, recip


def norm_backward(grad_out, normal_part, recip, gain_vec):
    scaled = grad_out * gain_vec
    return recip * (
        scaled
        - jnp.mean(scaled, -1, keepdims=True)
        - normal_part * jnp.mean(scaled * normal_part, -1, keepdims=True)
    )


def dot(a, b):
    return jnp.dot(a, b, preferred_element_type=F32)


def dot_nt(a, b):
    return lax.dot_general(a, b, (((1,), (1,)), ((), ())), preferred_element_type=F32)


def dot_tn(a, b):
    return lax.dot_general(a, b, (((0,), (0,)), ((), ())), preferred_element_type=F32)


def pad_rows(a):
    return jnp.pad(a, ((0, PAD - a.shape[0]), (0, 0)))


def block_of(a, j):
    return lax.dynamic_slice_in_dim(a, j * BLK, BLK, 0)


def exchange(a, axis):
    return lax.all_to_all(a, axis, 0, 0, tiled=True)


def gather(piece):
    return exchange(jnp.broadcast_to(piece[None], (NT,) + piece.shape), T)


def hop(a, mask):
    return lax.ppermute(a, DP, [(i, i ^ mask) for i in range(16)])


def tensor_hop(a, mask):
    return lax.ppermute(a, T, [(i, i ^ mask) for i in range(NT)])


def pick(a, j, axis=0):
    return lax.dynamic_index_in_dim(a, j, axis, keepdims=False)


def place(dp):
    return dp % 2, (dp // 2) % 4, dp // 8


def z_add(two, got):
    return (two.astype(F32) + got.astype(F32)).astype(BF)


def y_spread(by_z):
    return tuple(hop(by_z, 2 * k) for k in (1, 2, 3))


def spread(where_ref, own_ref, other_ref, left_ref, right_ref):
    chunk = own_ref.shape[2]
    cut = left_ref.shape[1]
    core, y = where_ref[0], where_ref[1]
    for c in range(2):
        for z in range(2):
            for pair in (0, 2):
                parts = []
                for j in (pair, pair + 1):
                    a, b = own_ref[y ^ j, z], other_ref[y ^ j, z]
                    parts.append(jnp.where(core == c, a, b))
                rows = jnp.concatenate(parts, 0)
                lo = (c * 8 + z * 4 + pair) * chunk
                left_ref[lo : lo + 2 * chunk, :] = rows[:, :cut].astype(F32)
                right_ref[:, lo : lo + 2 * chunk] = jnp.transpose(rows[:, cut:]).astype(F32)


def natural_chunks(own, other, dp, cut):
    core, y, _ = place(dp)
    n, chunk, width = 16, own.shape[2], own.shape[3]
    return pl.pallas_call(
        spread,
        out_shape=[shaped(n * chunk, cut), shaped(width - cut, n * chunk)],
        in_specs=[SMEM_SPEC] + whole(2),
        out_specs=whole(2),
        compiler_params=BIG,
        cost_estimate=SHORT,
    )(jnp.stack([core, y]).astype(jnp.int32), *far(own, other))


def attend_forward(
    where_ref, hid_ref, gain_ref, shift_ref, w_ref, qb_ref, vb_ref, srow_ref, scol_ref,
    act_ref, qkv_ref, ctx_ref, send_ref, lse_ref,
):
    seq_len = hid_ref.shape[0]
    for lo, hi in row_blocks(seq_len):
        xhat, _ = norm_stats(hid_ref[lo:hi, :])
        act_ref[lo:hi, :] = (xhat * gain_ref[...] + shift_ref[...]).astype(BF)
    none = jnp.zeros((1, HEAD_DIM), F32)
    cut = HEAD_DIM
    bias = jnp.concatenate(
        [qb_ref[:, :cut], none, vb_ref[:, :cut], qb_ref[:, cut:], none, vb_ref[:, cut:]], 1
    )
    for lo, hi in halves(seq_len):
        qkv_ref[lo:hi, :] = (dot(act_ref[lo:hi, :], w_ref[...]) + bias).astype(BF)
    even = where_ref[1] == 0
    slopes = head_slopes(where_ref)
    for lo, hi in row_blocks(seq_len):
        allowed, distance = masks(lo, hi, srow_ref, scol_ref)
        outs = []
        for h in range(2):
            s = head_scores(qkv_ref, slopes, h, lo, hi, allowed, distance)
            top = jnp.max(s, -1, keepdims=True)
            e = jnp.exp(s - top)
            total = jnp.sum(e, -1, keepdims=True)
            lse_ref[h, lo:hi, :] = top + jnp.log(total)
            p = (e / total).astype(BF)
            outs.append(dot(p, qkv_ref[:hi, head_part(h, 2)]).astype(BF))
        ctx_ref[lo:hi, :] = jnp.concatenate(outs, 1)
        first = jnp.where(even, outs[0].astype(F32), outs[1].astype(F32))
        second = jnp.where(even, outs[1].astype(F32), outs[0].astype(F32))
        both = jnp.concatenate([first, second], 1).astype(BF)
        for i in range(NT):
            send_ref[i, lo:hi, :] = both
    pad = jnp.zeros((PAD - seq_len, 2 * HEAD_DIM), BF)
    for i in range(NT):
        send_ref[i, seq_len:, :] = pad


def row_blocks(n):
    return [(lo, min(lo + 128, n)) for lo in range(0, n, 128)]


def halves(n):
    return [(0, 304), (304, n)]


def head_part(h, c):
    start = (h * 3 + c) * HEAD_DIM
    return slice(start, start + HEAD_DIM)


def head_slopes(where_ref):
    first = (where_ref[0] * 2).astype(F32)
    return [
        jnp.exp2(jnp.full((1, 1), -(8.0 / HEADS), F32) * (first + (h + 1.0))) for h in range(2)
    ]


def masks(lo, hi, srow_ref, scol_ref):
    shape = (hi - lo, hi)
    diff = lax.broadcasted_iota(jnp.int32, shape, 1) - lax.broadcasted_iota(jnp.int32, shape, 0) - lo
    allowed = (diff <= 0) & (scol_ref[lo:hi, :] == srow_ref[:, :hi])
    return allowed, diff.astype(F32)


def head_scores(qkv_ref, slopes, h, lo, hi, allowed, distance):
    raw = dot_nt(qkv_ref[lo:hi, head_part(h, 0)], qkv_ref[:hi, head_part(h, 1)])
    return jnp.where(allowed, raw * HEAD_DIM ** (-0.5) + slopes[h] * distance, NEG)


def attend_backward(
    where_ref, branch_ref, wd_ref, qkv_ref, lse_ref, srow_ref, scol_ref, w_ref,
    grad_ref, part_ref, acc_ref, cg_ref,
):
    seq_len = qkv_ref.shape[0]
    scale = HEAD_DIM ** (-0.5)
    for i in (0, 4):
        rows = jnp.concatenate([branch_ref[j, :BLK, :] for j in range(i, i + 4)], 0)
        cg_ref[i * BLK : (i + 4) * BLK, :] = dot_nt(rows, wd_ref[...]).astype(BF)
    total = branch_ref[0, BLK:, :].astype(F32)
    for j in range(1, NT):
        total = total + branch_ref[j, BLK:, :].astype(F32)
    total = total.astype(BF)
    for j in range(NT):
        part_ref[j, BLK:, :] = total
    acc_ref[...] = jnp.zeros_like(acc_ref)
    slopes = head_slopes(where_ref)
    for lo, hi in row_blocks(seq_len):
        allowed, distance = masks(lo, hi, srow_ref, scol_ref)
        cg_all = cg_ref[lo:hi, :]
        for h in range(2):
            s = head_scores(qkv_ref, slopes, h, lo, hi, allowed, distance)
            p = jnp.exp(s - lse_ref[h, lo:hi, :])
            cg = cg_all[:, h * HEAD_DIM : (h + 1) * HEAD_DIM]
            pg = dot_nt(cg, qkv_ref[:hi, head_part(h, 2)])
            acc_ref[2 * h + 1, :, :hi] += dot_tn(cg, p.astype(BF))
            sg = (p * (pg - jnp.sum(pg * p, -1, keepdims=True))).astype(BF)
            grad_ref[lo:hi, head_part(h, 0)] = (
                dot(sg, qkv_ref[:hi, head_part(h, 1)]) * scale
            ).astype(BF)
            acc_ref[2 * h, :, :hi] += dot_tn(qkv_ref[lo:hi, head_part(h, 0)], sg)
    for h in range(2):
        kg = jnp.transpose(acc_ref[2 * h, :, :]) * scale
        vg = jnp.transpose(acc_ref[2 * h + 1, :, :])
        grad_ref[:, head_part(h, 1)] = kg.astype(BF)
        grad_ref[:, head_part(h, 2)] = vg.astype(BF)
    for h in range(2):
        grad_ref[seq_len:, head_part(h, 0)] = jnp.zeros((PAD - seq_len, HEAD_DIM), BF)
    for lo in range(0, PAD, 320):
        part = dot_nt(grad_ref[lo : lo + 320, :], w_ref[...]).astype(BF)
        for j in range(4):
            part_ref[lo // BLK + j, :BLK, :] = part[j * BLK : (j + 1) * BLK, :]


def feed(
    ctx_ref, own_ref, other_ref, hid_ref, db_ref, gain_ref, shift_ref, up_ref, ub_ref, gin_ref,
    mid_ref, act_ref, gelu_ref, low_ref, part_ref, sum_ref,
):
    step = pl.program_id(0)
    ctx_a = jnp.concatenate([ctx_ref[i, :, :HEAD_DIM] for i in range(NT)], 1)
    ctx_b = jnp.concatenate([ctx_ref[i, :, HEAD_DIM:] for i in range(NT)], 1)
    attn = dot(ctx_a, own_ref[...]) + dot(ctx_b, other_ref[...])
    middle = hid_ref[...] + (attn + db_ref[...])
    mid_ref[...] = middle
    xhat, _ = norm_stats(middle)
    act = (xhat * gain_ref[...] + shift_ref[...]).astype(BF)
    act_ref[...] = act
    x = dot(act, up_ref[...]) + ub_ref[...]
    a = 0.7978845608028654
    t = jnp.tanh(a * (x + 0.044715 * x * x * x))
    gelu_ref[...] = (x * (0.5 * (1.0 + t))).astype(BF)
    slope = 0.5 * (1.0 + t) + 0.5 * x * (1.0 - t * t) * (a * (1.0 + 3 * 0.044715 * x * x))
    low = (gin_ref[...] * slope).astype(BF)
    low_ref[...] = low
    part_ref[...] = dot_nt(low, up_ref[...]).astype(BF)

    @pl.when(step == 0)
    def _():
        sum_ref[...] = jnp.zeros_like(sum_ref)

    sum_ref[...] += jnp.sum(low.astype(F32), 0, keepdims=True)


def norm_two_back(
    me_ref, got_ref, mid_ref, og_ref, gain_ref, mlp_ref, back_ref, send_ref, sum_ref
):
    total = got_ref[0].astype(F32)
    for i in range(1, NT):
        total = total + got_ref[i].astype(F32)
    xhat, recip = norm_stats(mid_ref[...])
    back = norm_backward(total, xhat, recip, gain_ref[...])
    back_ref[...] = back
    branch = (og_ref[...] + back).astype(BF)
    for i in range(NT):
        send_ref[i, :BLK, :] = branch
        send_ref[i, BLK:, :] = mlp_ref[i]
    sum_ref[0:1, :] = jnp.sum(total * xhat, 0, keepdims=True)
    sum_ref[1:2, :] = jnp.sum(total, 0, keepdims=True)
    sum_ref[2:3, :] = jnp.sum(branch.astype(F32), 0, keepdims=True)
    sum_ref[3:8, :] = jnp.zeros((5, sum_ref.shape[1]), F32)


def norm_one_back(me_ref, got_ref, hid_ref, back_ref, gain_ref, vec_ref, send_ref):
    total = got_ref[0].astype(F32)
    for i in range(1, NT):
        total = total + got_ref[i].astype(F32)
    xhat, recip = norm_stats(hid_ref[...])
    delta = (back_ref[...] + norm_backward(total, xhat, recip, gain_ref[...])).astype(BF)
    pairs = [vec_ref[2 * i : 2 * i + 2, :] for i in range(8)]
    vec = jnp.concatenate([jnp.concatenate([p[:1], p[1:]], 1) for p in pairs], 0)
    both = jnp.concatenate(split(vec), 0)
    for i in range(NT):
        send_ref[i, :BLK, :] = delta
        send_ref[i, BLK:, :] = both


def mlp_out(gelu_ref, w_ref, out_ref):
    for lo in (0, 320):
        out_ref[lo : lo + 320, :] = dot(gelu_ref[lo : lo + 320, :], w_ref[...]).astype(BF)


def early_grads(where_ref, act_ref, low_ref, grad_ref, gelu_ref, keep_ref, give_ref, sum_ref):
    half = keep_ref.shape[0]
    for ref, side in ((keep_ref, where_ref[1]), (give_ref, 1 - where_ref[1])):
        cols = pl.ds(pl.multiple_of(side * half, half), half)
        ref[:, :512] = dot_tn(act_ref[:, cols], low_ref[...]).astype(BF)
        ref[:, 512:] = dot_tn(grad_ref[:, cols], gelu_ref[...]).astype(BF)
    sum_ref[...] = jnp.sum(grad_ref[...].astype(F32), 0, keepdims=True)


def split(v):
    high = v.astype(BF)
    return high, (v - high.astype(F32)).astype(BF)


def join(high, low):
    return high.astype(F32) + low.astype(F32)


def late_grads(
    where_ref, act_ref, grad_ref, branch_ref, ctx_ref, part_ref, hid_ref, two_ref, up_ref,
    down_ref, keep_ref, give_ref, vec_ref,
):
    seq_len, width = act_ref.shape
    half = width // 2
    for ref, side in ((keep_ref, where_ref[1]), (give_ref, 1 - where_ref[1])):
        cols = pl.ds(pl.multiple_of(side * half, half), half)
        ref[:half, :384] = dot_tn(act_ref[:, cols], grad_ref[:seq_len, :]).astype(BF)
        branch = jnp.concatenate([branch_ref[j, :BLK, cols] for j in range(NT)], 0)
        ref[:half, 384:] = dot_tn(branch[:seq_len], ctx_ref[...]).astype(BF)
    gain = jnp.zeros((1, width), F32)
    shift = gain
    for j in range(NT):
        lo, hi = j * BLK, min(j * BLK + BLK, seq_len)
        xhat, _ = norm_stats(hid_ref[lo:hi, :])
        part = part_ref[j, : hi - lo, :].astype(F32)
        gain = gain + jnp.sum(part * xhat, 0, keepdims=True)
        shift = shift + jnp.sum(part, 0, keepdims=True)
    sums = jnp.sum(grad_ref[...].astype(F32), 0, keepdims=True)
    last = jnp.concatenate([up_ref[...], sums, jnp.zeros((1, 128), F32)], 1)
    vectors = [
        gain, shift, two_ref[0:1, :], two_ref[1:2, :], two_ref[2:3, :], down_ref[...], last,
        jnp.zeros_like(last),
    ]
    for i, v in enumerate(vectors):
        vec_ref[2 * i : 2 * i + 1, :] = v[:, :half]
        vec_ref[2 * i + 1 : 2 * i + 2, :] = v[:, half:]
    high, low = split(vec_ref[...])
    give_ref[half : half + 16, :] = high
    give_ref[half + 16 :, :] = low


def early_core(where_ref, keep_ref, got_ref, own_ref, one_ref, two_ref, three_ref):
    y = where_ref[2]
    for k, ref in enumerate((own_ref, one_ref, two_ref, three_ref)):
        for z in range(2):
            total = keep_ref[z, y ^ k].astype(F32) + got_ref[z, y ^ k].astype(F32)
            ref[z] = total.astype(BF)


def late_core(
    where_ref, keep_ref, got_ref, vec_ref, own_ref, one_ref, two_ref, three_ref, out_ref
):
    y = where_ref[2]
    chunk = keep_ref.shape[2]
    half = 8 * chunk
    vec = vec_ref[...] + join(got_ref[half : half + 16, :], got_ref[half + 16 :, :])
    out_ref[...] = vec
    parts = split(vec)
    for k, ref in enumerate((own_ref, one_ref, two_ref, three_ref)):
        for z in range(2):
            rows = pl.ds(pl.multiple_of((z * 4 + (y ^ k)) * chunk, chunk), chunk)
            total = keep_ref[z, y ^ k].astype(F32) + got_ref[rows, :].astype(F32)
            ref[z, :chunk, :] = total.astype(BF)
            ref[z, chunk:, :] = parts[z]


def late_y(own_ref, one_ref, two_ref, three_ref, vec_ref, out_ref, sum_ref):
    chunk = own_ref.shape[1] - 16
    vec = vec_ref[...]
    for ref in (one_ref, two_ref, three_ref):
        vec = vec + join(ref[0, chunk:, :], ref[1, chunk:, :])
    sum_ref[...] = vec
    parts = split(vec)
    for z in range(2):
        total = own_ref[z, :chunk, :].astype(F32)
        for ref in (one_ref, two_ref, three_ref):
            total = total + ref[z, :chunk, :].astype(F32)
        out_ref[z, :chunk, :] = total.astype(BF)
        out_ref[z, chunk:, :] = parts[z]


def late_z(own_ref, got_ref, vec_ref, out_ref, down_ref, up_ref, query_ref, value_ref):
    chunk = out_ref.shape[1]
    vec = vec_ref[...] + join(got_ref[0, chunk:, :], got_ref[1, chunk:, :])
    down_ref[...] = jnp.concatenate([vec[10:11], vec[11:12]], 1)
    up_ref[...] = vec[12:13]
    for ref, c in ((query_ref, 0), (value_ref, 2)):
        ref[...] = jnp.concatenate([vec[13:14, head_part(h, c)] for h in range(2)], 1)
    for z in range(2):
        total = own_ref[z, :chunk, :].astype(F32) + got_ref[z, :chunk, :].astype(F32)
        out_ref[z] = total.astype(BF)


def add_rows(mid_ref, got_ref, bias_ref, out_ref):
    for i in range(got_ref.shape[0]):
        rows = slice(i * BLK, (i + 1) * BLK)
        out_ref[rows, :] = mid_ref[rows, :] + (got_ref[i].astype(F32) + bias_ref[...])


def simple(kernel, outs, *args):
    return pl.pallas_call(
        kernel,
        out_shape=outs,
        in_specs=whole(len(args)),
        out_specs=whole(len(outs)),
        compiler_params=BIG,
        cost_estimate=TINY,
    )(*far(*args))


def late_call(where, *args):
    first = pl.BlockSpec((NT, BLK, 1024), lambda i: (0, 0, 0))
    full = lambda a: pl.BlockSpec(a.shape, lambda i: (0, 0))
    outs = [shaped(512, 512, dtype=BF), shaped(544, 512, dtype=BF), shaped(16, 512)]
    return pl.pallas_call(
        late_grads,
        grid=(1,),
        out_shape=outs,
        in_specs=[SMEM_SPEC] + [first if a.ndim == 3 else full(a) for a in args],
        out_specs=[pl.BlockSpec(o.shape, lambda i: (0, 0)) for o in outs],
        compiler_params=BIG,
        cost_estimate=LONG,
    )(where, *far(*args))


def simple_at(kernel, outs, where, *args, cost=None):
    return pl.pallas_call(
        kernel,
        out_shape=outs,
        in_specs=[SMEM_SPEC] + whole(len(args)),
        out_specs=whole(len(outs)),
        compiler_params=BIG,
        cost_estimate=cost or TINY,
    )(where, *far(*args))


def whole(n):
    return [pl.BlockSpec(memory_space=pltpu.VMEM)] * n


SMEM_SPEC = pl.BlockSpec(memory_space=pltpu.SMEM)
LONG = pl.CostEstimate(flops=4 << 30, bytes_accessed=24 << 20, transcendentals=0)
SHORT = pl.CostEstimate(flops=1 << 20, bytes_accessed=10 << 20, transcendentals=0)
TINY = pl.CostEstimate(flops=1, bytes_accessed=1, transcendentals=0)
BIG = pltpu.CompilerParams(vmem_limit_bytes=40 << 20)


def shaped(*shape, dtype=F32):
    return pltpu.HBM(shape, dtype)


def far(*arrays):
    return [pltpu.with_memory_space_constraint(a, pltpu.HBM) for a in arrays]


def tie(*arrays):
    return lax.optimization_barrier(arrays)


def per_device(
    hidden_in,
    segments,
    ln1_gain,
    ln1_shift,
    qkv_weight,
    query_bias,
    value_bias,
    dense_weight,
    dense_bias,
    ln2_gain,
    ln2_shift,
    up_weight,
    up_bias,
    down_weight,
    down_bias,
    out_grad,
):
    seq_len, width = hidden_in.shape
    me = lax.axis_index(T)
    dp = lax.axis_index(DP)
    core = dp % 2
    row = lambda v: v.reshape(1, -1)
    where = jnp.stack([me, core, (dp // 2) % 4]).astype(jnp.int32)

    half_w = lax.dynamic_slice_in_dim(dense_weight, core * HEAD_DIM, HEAD_DIM, 0)
    own_w = gather(half_w).reshape(NT * HEAD_DIM, width)
    other_w = hop(own_w, 1)

    seg_col = segments.reshape(seq_len, 1)
    act_one, qkv_low, context, ctx_send, lse = pl.pallas_call(
        attend_forward,
        out_shape=[
            shaped(seq_len, width, dtype=BF),
            shaped(seq_len, 384, dtype=BF),
            shaped(seq_len, 128, dtype=BF),
            shaped(NT, PAD, 128, dtype=BF),
            shaped(2, seq_len, 1),
        ],
        in_specs=[SMEM_SPEC] + whole(8),
        out_specs=whole(5),
        compiler_params=BIG,
        cost_estimate=LONG,
    )(
        where,
        *far(hidden_in),
        row(ln1_gain),
        row(ln1_shift),
        *far(qkv_weight),
        row(query_bias),
        row(value_bias),
        segments,
        seg_col,
    )
    ctx_got = exchange(ctx_send, T)

    grad_pad = pad_rows(out_grad.astype(BF))
    gelu_in_grad = dot_nt(grad_pad, down_weight)
    hid_pad = pad_rows(hidden_in)
    out_grad_pad = pad_rows(out_grad)

    rows = 320
    tile = lambda w: pl.BlockSpec((rows, w), lambda i: (i, 0))
    fixed = lambda *shape: pl.BlockSpec(shape, lambda i: (0,) * len(shape))
    middle, act_two, gelu_low, up_low, norm_two_part, up_bias_part = pl.pallas_call(
        feed,
        grid=(PAD // rows,),
        out_shape=[
            shaped(PAD, width),
            shaped(PAD, width, dtype=BF),
            shaped(PAD, 512, dtype=BF),
            shaped(PAD, 512, dtype=BF),
            shaped(PAD, width, dtype=BF),
            shaped(1, 512),
        ],
        in_specs=[
            pl.BlockSpec((NT, rows, 128), lambda i: (0, i, 0)),
            fixed(512, width),
            fixed(512, width),
            tile(width),
            fixed(1, width),
            fixed(1, width),
            fixed(1, width),
            fixed(width, 512),
            fixed(1, 512),
            tile(512),
        ],
        out_specs=[tile(width), tile(width), tile(512), tile(512), tile(width), fixed(1, 512)],
        compiler_params=BIG,
        cost_estimate=TINY,
    )(
        *far(ctx_got, own_w, other_w, hid_pad),
        row(dense_bias),
        row(ln2_gain),
        row(ln2_shift),
        *far(up_weight),
        row(up_bias),
        *far(gelu_in_grad),
    )
    two_got = exchange(norm_two_part.reshape(NT, BLK, width), T)

    mlp_part = pl.pallas_call(
        mlp_out,
        out_shape=shaped(PAD, width, dtype=BF),
        in_specs=whole(2),
        out_specs=whole(1)[0],
        compiler_params=BIG,
        cost_estimate=TINY,
    )(*far(gelu_low, down_weight))
    e_keep, e_give, down_bias_part = simple_at(
        early_grads,
        [shaped(512, width, dtype=BF), shaped(512, width, dtype=BF), shaped(1, width)],
        where, act_two, up_low, grad_pad, gelu_low,
    )
    e_core = hop(e_give, 1)
    two_got, e_core, mlp_part = tie(two_got, e_core, mlp_part)

    mine = pl.BlockSpec((BLK, width), lambda i, m: (m[0], 0))
    zero = lambda *shape: pl.BlockSpec(shape, lambda i, m: (0,) * len(shape))
    back_two, branch_send, sums_two = pl.pallas_call(
        norm_two_back,
        out_shape=[shaped(BLK, width), shaped(NT, 2 * BLK, width, dtype=BF), shaped(8, width)],
        grid_spec=pltpu.PrefetchScalarGridSpec(
            num_scalar_prefetch=1,
            grid=(1,),
            in_specs=[
                zero(NT, BLK, width), mine, mine, zero(1, width), zero(NT, BLK, width)
            ],
            out_specs=[zero(BLK, width), zero(NT, 2 * BLK, width), zero(8, width)],
        ),
        compiler_params=BIG,
        cost_estimate=TINY,
    )(
        me.reshape(1),
        *far(two_got, middle, out_grad_pad),
        row(ln2_gain),
        *far(mlp_part.reshape(NT, BLK, width)),
    )
    branch = exchange(branch_send, T)

    e_core, branch_send = tie(e_core, branch_send)
    e_own, *e_y = simple_at(
        early_core,
        [shaped(2, 64, width, dtype=BF)] * 4,
        where, e_keep.reshape(2, 4, 64, width), e_core.reshape(2, 4, 64, width),
    )
    e_y = tie(*[hop(e, 2 * (k + 1)) for k, e in enumerate(e_y)])
    e_two = sum([e.astype(F32) for e in e_y], e_own.astype(F32)).astype(BF)
    branch, e_two = tie(branch, e_two)
    e_z = hop(e_two, 8)

    qkv_grad_low, norm_one_part = pl.pallas_call(
        attend_backward,
        out_shape=[shaped(PAD, 384, dtype=BF), shaped(NT, 2 * BLK, width, dtype=BF)],
        in_specs=[SMEM_SPEC] + whole(7),
        out_specs=whole(2),
        scratch_shapes=[pltpu.VMEM((4, HEAD_DIM, PAD), F32), pltpu.VMEM((PAD, 128), BF)],
        compiler_params=BIG,
        cost_estimate=LONG,
    )(where, *far(branch, dense_weight, qkv_low, lse), segments, seg_col, *far(qkv_weight))
    norm_one_part, e_z = tie(norm_one_part, e_z)
    one_got = exchange(norm_one_part, T)

    e_three = z_add(e_two, e_z)
    e_y = y_spread(e_three)
    l_keep, l_give, vec = late_call(
        where, act_one, qkv_grad_low, branch, context, norm_one_part, hidden_in, sums_two,
        up_bias_part, down_bias_part,
    )
    l_give, *e_y = tie(l_give, *e_y)
    l_core = hop(l_give, 1)
    l_own, *l_y, vec = simple_at(
        late_core,
        [shaped(2, 80, 512, dtype=BF)] * 4 + [shaped(16, 512)],
        where, l_keep.reshape(2, 4, 64, 512), l_core, vec,
    )
    e_by_y = jnp.stack([e_three, *e_y])
    e_core, *l_y = tie(hop(e_by_y, 1), *[hop(p, 2 * (k + 1)) for k, p in enumerate(l_y)])
    l_two, vec = simple(
        late_y, [shaped(2, 80, 512, dtype=BF), shaped(16, 512)], l_own, *l_y, vec
    )
    one_got, l_two, vec, e_core, e_by_y = tie(one_got, l_two, vec, e_core, e_by_y)
    l_z = hop(l_two, 8)

    in_send = pl.pallas_call(
        norm_one_back,
        out_shape=shaped(NT, BLK + 16, width, dtype=BF),
        grid_spec=pltpu.PrefetchScalarGridSpec(
            num_scalar_prefetch=1,
            grid=(1,),
            in_specs=[
                zero(NT, BLK, width), mine, zero(BLK, width), zero(1, width), zero(16, 512)
            ],
            out_specs=zero(NT, BLK + 16, width),
        ),
        compiler_params=BIG,
        cost_estimate=LONG,
    )(me.reshape(1), *far(one_got, hid_pad, back_two), row(ln1_gain), *far(vec))
    in_send, l_z, one_got, e_core, e_by_y = tie(in_send, l_z, one_got, e_core, e_by_y)
    in_got = exchange(in_send, T)

    l_three, down_bias_grad, up_bias_grad, query_bias_grad, value_bias_grad = simple(
        late_z,
        [shaped(2, 64, 512, dtype=BF)] + [shaped(1, n) for n in (width, 512, 128, 128)],
        l_two, l_z, vec,
    )
    up_weight_grad, down_weight_grad = natural_chunks(e_by_y, e_core, dp, 512)
    block_out = pl.pallas_call(
        add_rows,
        grid=(NT // 4,),
        out_shape=shaped(seq_len, width),
        in_specs=[
            pl.BlockSpec((4 * BLK, width), lambda i: (i, 0)),
            pl.BlockSpec((4, BLK, width), lambda i: (i, 1, 0)),
            fixed(1, width),
        ],
        out_specs=pl.BlockSpec((4 * BLK, width), lambda i: (i, 0)),
        compiler_params=BIG,
        cost_estimate=SHORT,
    )(*far(middle, one_got), row(down_bias))
    up_weight_grad, block_out, *l_y = tie(up_weight_grad, block_out, *y_spread(l_three))
    l_by_y = jnp.stack([l_three, *l_y])
    l_core = hop(l_by_y, 1)
    qkv_weight_grad, dense_weight_grad = natural_chunks(l_by_y, l_core, dp, 384)
    in_got, qkv_weight_grad = tie(in_got, qkv_weight_grad)
    shared = jnp.sum(in_got[:, BLK : BLK + 8].astype(F32) + in_got[:, BLK + 8 :].astype(F32), 0)
    shared = shared + hop(shared, 8)
    input_grad = out_grad + in_got[:, :BLK].reshape(PAD, width)[:seq_len].astype(F32)
    return (
        block_out,
        input_grad,
        shared[0],
        shared[1],
        qkv_weight_grad,
        query_bias_grad[0],
        value_bias_grad[0],
        dense_weight_grad,
        shared[4],
        shared[2],
        shared[3],
        up_weight_grad,
        up_bias_grad[0],
        down_weight_grad,
        down_bias_grad[0],
    )


def solution(mesh):
    placed = (
        P("dp", None),
        P("dp", None),
        P(),
        P(),
        P(None, "tensor"),
        P("tensor"),
        P("tensor"),
        P("tensor", None),
        P(),
        P(),
        P(),
        P(None, "tensor"),
        P("tensor"),
        P("tensor", None),
        P(),
        P("dp", None),
    )
    return jax.shard_map(
        per_device,
        mesh=mesh,
        in_specs=placed,
        out_specs=(
            P("dp", None),
            P("dp", None),
            P(),
            P(),
            P(None, "tensor"),
            P("tensor"),
            P("tensor"),
            P("tensor", None),
            P(),
            P(),
            P(),
            P(None, "tensor"),
            P("tensor"),
            P("tensor", None),
            P(),
        ),
        check_vma=False,
    )
```

```python
from functools import partial

import jax
import jax.numpy as jnp
from jax import lax
from jax.experimental import pallas as pl
from jax.experimental.pallas import tpu as pltpu
from jax.sharding import PartitionSpec as P

HEADS = 16
HEAD_DIM = 64
EPS = 1e-05
NEG = -1000000000.0
T = "tensor"
DP = "dp"
NT = 8
BLK = 80
PAD = NT * BLK
BF = jnp.bfloat16
F32 = jnp.float32


def norm_stats(values_in):
    row_mean = jnp.mean(values_in, -1, keepdims=True)
    centred = values_in - row_mean
    variance = jnp.mean(centred * centred, -1, keepdims=True)
    recip = lax.rsqrt(variance + EPS)
    return centred * recip, recip


def norm_backward(grad_out, normal_part, recip, gain_vec):
    scaled = grad_out * gain_vec
    return recip * (
        scaled
        - jnp.mean(scaled, -1, keepdims=True)
        - normal_part * jnp.mean(scaled * normal_part, -1, keepdims=True)
    )


def dot(a, b):
    return jnp.dot(a, b, preferred_element_type=F32)


def dot_nt(a, b):
    return lax.dot_general(a, b, (((1,), (1,)), ((), ())), preferred_element_type=F32)


def dot_tn(a, b):
    return lax.dot_general(a, b, (((0,), (0,)), ((), ())), preferred_element_type=F32)


def pad_rows(a):
    return jnp.pad(a, ((0, PAD - a.shape[0]), (0, 0)))


def block_of(a, j):
    return lax.dynamic_slice_in_dim(a, j * BLK, BLK, 0)


def exchange(a, axis):
    return lax.all_to_all(a, axis, 0, 0, tiled=True)


def gather(piece):
    return exchange(jnp.broadcast_to(piece[None], (NT,) + piece.shape), T)


def hop(a, mask):
    return lax.ppermute(a, DP, [(i, i ^ mask) for i in range(16)])


def tensor_hop(a, mask):
    return lax.ppermute(a, T, [(i, i ^ mask) for i in range(NT)])


def pick(a, j, axis=0):
    return lax.dynamic_index_in_dim(a, j, axis, keepdims=False)


def place(dp):
    return dp % 2, (dp // 2) % 4, dp // 8


def z_add(two, got):
    return (two.astype(F32) + got.astype(F32)).astype(BF)


def y_spread(by_z):
    return tuple(hop(by_z, 2 * k) for k in (1, 2, 3))


def spread(where_ref, own_ref, other_ref, left_ref, right_ref):
    chunk = own_ref.shape[2]
    cut = left_ref.shape[1]
    core, y = where_ref[0], where_ref[1]
    for c in range(2):
        for z in range(2):
            for pair in (0, 2):
                parts = []
                for j in (pair, pair + 1):
                    a, b = own_ref[y ^ j, z], other_ref[y ^ j, z]
                    parts.append(jnp.where(core == c, a, b))
                rows = jnp.concatenate(parts, 0)
                lo = (c * 8 + z * 4 + pair) * chunk
                left_ref[lo : lo + 2 * chunk, :] = rows[:, :cut].astype(F32)
                right_ref[:, lo : lo + 2 * chunk] = jnp.transpose(rows[:, cut:]).astype(F32)


def natural_chunks(own, other, dp, cut):
    core, y, _ = place(dp)
    n, chunk, width = 16, own.shape[2], own.shape[3]
    return pl.pallas_call(
        spread,
        out_shape=[shaped(n * chunk, cut), shaped(width - cut, n * chunk)],
        in_specs=[SMEM_SPEC] + whole(2),
        out_specs=whole(2),
        compiler_params=BIG,
        cost_estimate=SHORT,
    )(jnp.stack([core, y]).astype(jnp.int32), *far(own, other))


def attend_forward(
    where_ref, hid_ref, gain_ref, shift_ref, w_ref, qb_ref, vb_ref, srow_ref, scol_ref,
    act_ref, qkv_ref, ctx_ref, send_ref, lse_ref,
):
    seq_len = hid_ref.shape[0]
    for lo, hi in row_blocks(seq_len):
        xhat, _ = norm_stats(hid_ref[lo:hi, :])
        act_ref[lo:hi, :] = (xhat * gain_ref[...] + shift_ref[...]).astype(BF)
    none = jnp.zeros((1, HEAD_DIM), F32)
    cut = HEAD_DIM
    bias = jnp.concatenate(
        [qb_ref[:, :cut], none, vb_ref[:, :cut], qb_ref[:, cut:], none, vb_ref[:, cut:]], 1
    )
    for lo, hi in halves(seq_len):
        qkv_ref[lo:hi, :] = (dot(act_ref[lo:hi, :], w_ref[...]) + bias).astype(BF)
    even = where_ref[1] == 0
    slopes = head_slopes(where_ref)
    for lo, hi in row_blocks(seq_len):
        allowed, distance = masks(lo, hi, srow_ref, scol_ref)
        outs = []
        for h in range(2):
            s = head_scores(qkv_ref, slopes, h, lo, hi, allowed, distance)
            top = jnp.max(s, -1, keepdims=True)
            e = jnp.exp(s - top)
            total = jnp.sum(e, -1, keepdims=True)
            lse_ref[h, lo:hi, :] = top + jnp.log(total)
            p = (e / total).astype(BF)
            outs.append(dot(p, qkv_ref[:hi, head_part(h, 2)]).astype(BF))
        ctx_ref[lo:hi, :] = jnp.concatenate(outs, 1)
        first = jnp.where(even, outs[0].astype(F32), outs[1].astype(F32))
        second = jnp.where(even, outs[1].astype(F32), outs[0].astype(F32))
        both = jnp.concatenate([first, second], 1).astype(BF)
        for i in range(NT):
            send_ref[i, lo:hi, :] = both
    pad = jnp.zeros((PAD - seq_len, 2 * HEAD_DIM), BF)
    for i in range(NT):
        send_ref[i, seq_len:, :] = pad


def row_blocks(n):
    return [(lo, min(lo + 128, n)) for lo in range(0, n, 128)]


def halves(n):
    return [(0, 304), (304, n)]


def head_part(h, c):
    start = (h * 3 + c) * HEAD_DIM
    return slice(start, start + HEAD_DIM)


def head_slopes(where_ref):
    first = (where_ref[0] * 2).astype(F32)
    return [
        jnp.exp2(jnp.full((1, 1), -(8.0 / HEADS), F32) * (first + (h + 1.0))) for h in range(2)
    ]


def masks(lo, hi, srow_ref, scol_ref):
    shape = (hi - lo, hi)
    diff = lax.broadcasted_iota(jnp.int32, shape, 1) - lax.broadcasted_iota(jnp.int32, shape, 0) - lo
    allowed = (diff <= 0) & (scol_ref[lo:hi, :] == srow_ref[:, :hi])
    return allowed, diff.astype(F32)


def head_scores(qkv_ref, slopes, h, lo, hi, allowed, distance):
    raw = dot_nt(qkv_ref[lo:hi, head_part(h, 0)], qkv_ref[:hi, head_part(h, 1)])
    return jnp.where(allowed, raw * HEAD_DIM ** (-0.5) + slopes[h] * distance, NEG)


def attend_backward(
    where_ref, branch_ref, wd_ref, qkv_ref, lse_ref, srow_ref, scol_ref, w_ref,
    grad_ref, part_ref, acc_ref, cg_ref,
):
    seq_len = qkv_ref.shape[0]
    scale = HEAD_DIM ** (-0.5)
    for i in (0, 4):
        rows = jnp.concatenate([branch_ref[j, :BLK, :] for j in range(i, i + 4)], 0)
        cg_ref[i * BLK : (i + 4) * BLK, :] = dot_nt(rows, wd_ref[...]).astype(BF)
    total = branch_ref[0, BLK:, :].astype(F32)
    for j in range(1, NT):
        total = total + branch_ref[j, BLK:, :].astype(F32)
    total = total.astype(BF)
    for j in range(NT):
        part_ref[j, BLK:, :] = total
    acc_ref[...] = jnp.zeros_like(acc_ref)
    slopes = head_slopes(where_ref)
    for lo, hi in row_blocks(seq_len):
        allowed, distance = masks(lo, hi, srow_ref, scol_ref)
        cg_all = cg_ref[lo:hi, :]
        for h in range(2):
            s = head_scores(qkv_ref, slopes, h, lo, hi, allowed, distance)
            p = jnp.exp(s - lse_ref[h, lo:hi, :])
            cg = cg_all[:, h * HEAD_DIM : (h + 1) * HEAD_DIM]
            pg = dot_nt(cg, qkv_ref[:hi, head_part(h, 2)])
            acc_ref[2 * h + 1, :, :hi] += dot_tn(cg, p.astype(BF))
            sg = (p * (pg - jnp.sum(pg * p, -1, keepdims=True))).astype(BF)
            grad_ref[lo:hi, head_part(h, 0)] = (
                dot(sg, qkv_ref[:hi, head_part(h, 1)]) * scale
            ).astype(BF)
            acc_ref[2 * h, :, :hi] += dot_tn(qkv_ref[lo:hi, head_part(h, 0)], sg)
    for h in range(2):
        kg = jnp.transpose(acc_ref[2 * h, :, :]) * scale
        vg = jnp.transpose(acc_ref[2 * h + 1, :, :])
        grad_ref[:, head_part(h, 1)] = kg.astype(BF)
        grad_ref[:, head_part(h, 2)] = vg.astype(BF)
    for h in range(2):
        grad_ref[seq_len:, head_part(h, 0)] = jnp.zeros((PAD - seq_len, HEAD_DIM), BF)
    for lo in range(0, PAD, 320):
        part = dot_nt(grad_ref[lo : lo + 320, :], w_ref[...]).astype(BF)
        for j in range(4):
            part_ref[lo // BLK + j, :BLK, :] = part[j * BLK : (j + 1) * BLK, :]


def feed(
    ctx_ref, own_ref, other_ref, hid_ref, db_ref, gain_ref, shift_ref, up_ref, ub_ref, gin_ref,
    mid_ref, act_ref, gelu_ref, low_ref, part_ref, sum_ref,
):
    step = pl.program_id(0)
    ctx_a = jnp.concatenate([ctx_ref[i, :, :HEAD_DIM] for i in range(NT)], 1)
    ctx_b = jnp.concatenate([ctx_ref[i, :, HEAD_DIM:] for i in range(NT)], 1)
    attn = dot(ctx_a, own_ref[...]) + dot(ctx_b, other_ref[...])
    middle = hid_ref[...] + (attn + db_ref[...])
    mid_ref[...] = middle
    xhat, _ = norm_stats(middle)
    act = (xhat * gain_ref[...] + shift_ref[...]).astype(BF)
    act_ref[...] = act
    x = dot(act, up_ref[...]) + ub_ref[...]
    a = 0.7978845608028654
    t = jnp.tanh(a * (x + 0.044715 * x * x * x))
    gelu_ref[...] = (x * (0.5 * (1.0 + t))).astype(BF)
    slope = 0.5 * (1.0 + t) + 0.5 * x * (1.0 - t * t) * (a * (1.0 + 3 * 0.044715 * x * x))
    low = (gin_ref[...] * slope).astype(BF)
    low_ref[...] = low
    part_ref[...] = dot_nt(low, up_ref[...]).astype(BF)

    @pl.when(step == 0)
    def _():
        sum_ref[...] = jnp.zeros_like(sum_ref)

    sum_ref[...] += jnp.sum(low.astype(F32), 0, keepdims=True)


def norm_two_back(
    me_ref, got_ref, mid_ref, og_ref, gain_ref, mlp_ref, back_ref, send_ref, sum_ref
):
    total = got_ref[0].astype(F32)
    for i in range(1, NT):
        total = total + got_ref[i].astype(F32)
    xhat, recip = norm_stats(mid_ref[...])
    back = norm_backward(total, xhat, recip, gain_ref[...])
    back_ref[...] = back
    branch = (og_ref[...] + back).astype(BF)
    for i in range(NT):
        send_ref[i] = branch
    sum_ref[0:1, :] = jnp.sum(total * xhat, 0, keepdims=True)
    sum_ref[1:2, :] = jnp.sum(total, 0, keepdims=True)
    sum_ref[2:3, :] = jnp.sum(branch.astype(F32), 0, keepdims=True)
    sum_ref[3:8, :] = jnp.zeros((5, sum_ref.shape[1]), F32)


def norm_one_back(me_ref, got_ref, hid_ref, back_ref, gain_ref, vec_ref, send_ref):
    total = got_ref[0].astype(F32)
    for i in range(1, NT):
        total = total + got_ref[i].astype(F32)
    xhat, recip = norm_stats(hid_ref[...])
    delta = (back_ref[...] + norm_backward(total, xhat, recip, gain_ref[...])).astype(BF)
    pairs = [vec_ref[2 * i : 2 * i + 2, :] for i in range(8)]
    vec = jnp.concatenate([jnp.concatenate([p[:1], p[1:]], 1) for p in pairs], 0)
    both = jnp.concatenate(split(vec), 0)
    for i in range(NT):
        send_ref[i, :BLK, :] = delta
        send_ref[i, BLK:, :] = both


def mlp_out(gelu_ref, w_ref, out_ref):
    for lo in (0, 4):
        rows = slice(lo * BLK, (lo + 4) * BLK)
        part = dot(gelu_ref[rows, :], w_ref[...]).astype(BF)
        for j in range(4):
            out_ref[lo + j] = part[j * BLK : (j + 1) * BLK, :]


def early_grads(where_ref, act_ref, low_ref, grad_ref, gelu_ref, keep_ref, give_ref, sum_ref):
    half = keep_ref.shape[0]
    for ref, side in ((keep_ref, where_ref[1]), (give_ref, 1 - where_ref[1])):
        cols = pl.ds(pl.multiple_of(side * half, half), half)
        ref[:, :512] = dot_tn(act_ref[:, cols], low_ref[...]).astype(BF)
        ref[:, 512:] = dot_tn(grad_ref[:, cols], gelu_ref[...]).astype(BF)
    sum_ref[...] = jnp.sum(grad_ref[...].astype(F32), 0, keepdims=True)


def split(v):
    high = v.astype(BF)
    return high, (v - high.astype(F32)).astype(BF)


def join(high, low):
    return high.astype(F32) + low.astype(F32)


def late_grads(
    where_ref, act_ref, grad_ref, branch_ref, ctx_ref, part_ref, hid_ref, two_ref, up_ref,
    down_ref, keep_ref, give_ref, vec_ref,
):
    seq_len, width = act_ref.shape
    half = width // 2
    for ref, side in ((keep_ref, where_ref[1]), (give_ref, 1 - where_ref[1])):
        cols = pl.ds(pl.multiple_of(side * half, half), half)
        ref[:half, :384] = dot_tn(act_ref[:, cols], grad_ref[:seq_len, :]).astype(BF)
        branch = jnp.concatenate([branch_ref[j, :BLK, cols] for j in range(NT)], 0)
        ref[:half, 384:] = dot_tn(branch[:seq_len], ctx_ref[...]).astype(BF)
    gain = jnp.zeros((1, width), F32)
    shift = gain
    for j in range(NT):
        lo, hi = j * BLK, min(j * BLK + BLK, seq_len)
        xhat, _ = norm_stats(hid_ref[lo:hi, :])
        part = part_ref[j, : hi - lo, :].astype(F32)
        gain = gain + jnp.sum(part * xhat, 0, keepdims=True)
        shift = shift + jnp.sum(part, 0, keepdims=True)
    sums = jnp.sum(grad_ref[...].astype(F32), 0, keepdims=True)
    last = jnp.concatenate([up_ref[...], sums, jnp.zeros((1, 128), F32)], 1)
    vectors = [
        gain, shift, two_ref[0:1, :], two_ref[1:2, :], two_ref[2:3, :], down_ref[...], last,
        jnp.zeros_like(last),
    ]
    for i, v in enumerate(vectors):
        vec_ref[2 * i : 2 * i + 1, :] = v[:, :half]
        vec_ref[2 * i + 1 : 2 * i + 2, :] = v[:, half:]
    high, low = split(vec_ref[...])
    give_ref[half : half + 16, :] = high
    give_ref[half + 16 :, :] = low


def early_core(where_ref, keep_ref, got_ref, own_ref, one_ref, two_ref, three_ref):
    y = where_ref[2]
    for k, ref in enumerate((own_ref, one_ref, two_ref, three_ref)):
        for z in range(2):
            total = keep_ref[z, y ^ k].astype(F32) + got_ref[z, y ^ k].astype(F32)
            ref[z] = total.astype(BF)


def late_core(
    where_ref, keep_ref, got_ref, vec_ref, own_ref, one_ref, two_ref, three_ref, out_ref
):
    y = where_ref[2]
    chunk = keep_ref.shape[2]
    half = 8 * chunk
    vec = vec_ref[...] + join(got_ref[half : half + 16, :], got_ref[half + 16 :, :])
    out_ref[...] = vec
    parts = split(vec)
    for k, ref in enumerate((own_ref, one_ref, two_ref, three_ref)):
        for z in range(2):
            rows = pl.ds(pl.multiple_of((z * 4 + (y ^ k)) * chunk, chunk), chunk)
            total = keep_ref[z, y ^ k].astype(F32) + got_ref[rows, :].astype(F32)
            ref[z, :chunk, :] = total.astype(BF)
            ref[z, chunk:, :] = parts[z]


def late_y(own_ref, one_ref, two_ref, three_ref, vec_ref, out_ref, sum_ref):
    chunk = own_ref.shape[1] - 16
    vec = vec_ref[...]
    for ref in (one_ref, two_ref, three_ref):
        vec = vec + join(ref[0, chunk:, :], ref[1, chunk:, :])
    sum_ref[...] = vec
    parts = split(vec)
    for z in range(2):
        total = own_ref[z, :chunk, :].astype(F32)
        for ref in (one_ref, two_ref, three_ref):
            total = total + ref[z, :chunk, :].astype(F32)
        out_ref[z, :chunk, :] = total.astype(BF)
        out_ref[z, chunk:, :] = parts[z]


def late_z(own_ref, got_ref, vec_ref, out_ref, down_ref, up_ref, query_ref, value_ref):
    chunk = out_ref.shape[1]
    vec = vec_ref[...] + join(got_ref[0, chunk:, :], got_ref[1, chunk:, :])
    down_ref[...] = jnp.concatenate([vec[10:11], vec[11:12]], 1)
    up_ref[...] = vec[12:13]
    for ref, c in ((query_ref, 0), (value_ref, 2)):
        ref[...] = jnp.concatenate([vec[13:14, head_part(h, c)] for h in range(2)], 1)
    for z in range(2):
        total = own_ref[z, :chunk, :].astype(F32) + got_ref[z, :chunk, :].astype(F32)
        out_ref[z] = total.astype(BF)


def add_rows(mid_ref, got_ref, bias_ref, out_ref):
    for i in range(got_ref.shape[0]):
        rows = slice(i * BLK, (i + 1) * BLK)
        out_ref[rows, :] = mid_ref[rows, :] + (got_ref[i].astype(F32) + bias_ref[...])


def simple(kernel, outs, *args):
    return pl.pallas_call(
        kernel,
        out_shape=outs,
        in_specs=whole(len(args)),
        out_specs=whole(len(outs)),
        compiler_params=BIG,
        cost_estimate=TINY,
    )(*far(*args))


def late_call(where, *args):
    first = pl.BlockSpec((NT, BLK, 1024), lambda i: (0, 0, 0))
    full = lambda a: pl.BlockSpec(a.shape, lambda i: (0, 0))
    outs = [shaped(512, 512, dtype=BF), shaped(544, 512, dtype=BF), shaped(16, 512)]
    return pl.pallas_call(
        late_grads,
        grid=(1,),
        out_shape=outs,
        in_specs=[SMEM_SPEC] + [first if a.ndim == 3 else full(a) for a in args],
        out_specs=[pl.BlockSpec(o.shape, lambda i: (0, 0)) for o in outs],
        compiler_params=BIG,
        cost_estimate=LONG,
    )(where, *far(*args))


def simple_at(kernel, outs, where, *args, cost=None):
    return pl.pallas_call(
        kernel,
        out_shape=outs,
        in_specs=[SMEM_SPEC] + whole(len(args)),
        out_specs=whole(len(outs)),
        compiler_params=BIG,
        cost_estimate=cost or TINY,
    )(where, *far(*args))


def whole(n):
    return [pl.BlockSpec(memory_space=pltpu.VMEM)] * n


SMEM_SPEC = pl.BlockSpec(memory_space=pltpu.SMEM)
LONG = pl.CostEstimate(flops=4 << 30, bytes_accessed=24 << 20, transcendentals=0)
SHORT = pl.CostEstimate(flops=1 << 20, bytes_accessed=10 << 20, transcendentals=0)
TINY = pl.CostEstimate(flops=1, bytes_accessed=1, transcendentals=0)
BIG = pltpu.CompilerParams(vmem_limit_bytes=40 << 20)


def shaped(*shape, dtype=F32):
    return pltpu.HBM(shape, dtype)


def far(*arrays):
    return [pltpu.with_memory_space_constraint(a, pltpu.HBM) for a in arrays]


def tie(*arrays):
    return lax.optimization_barrier(arrays)


def per_device(
    hidden_in,
    segments,
    ln1_gain,
    ln1_shift,
    qkv_weight,
    query_bias,
    value_bias,
    dense_weight,
    dense_bias,
    ln2_gain,
    ln2_shift,
    up_weight,
    up_bias,
    down_weight,
    down_bias,
    out_grad,
):
    seq_len, width = hidden_in.shape
    me = lax.axis_index(T)
    dp = lax.axis_index(DP)
    core = dp % 2
    row = lambda v: v.reshape(1, -1)
    where = jnp.stack([me, core, (dp // 2) % 4]).astype(jnp.int32)

    part = HEAD_DIM // 2
    odd = (dp // 2) % 2
    piece = lax.dynamic_slice_in_dim(dense_weight, core * HEAD_DIM + odd * part, part, 0)
    piece = gather(piece)

    seg_col = segments.reshape(seq_len, 1)
    act_one, qkv_low, context, ctx_send, lse = pl.pallas_call(
        attend_forward,
        out_shape=[
            shaped(seq_len, width, dtype=BF),
            shaped(seq_len, 384, dtype=BF),
            shaped(seq_len, 128, dtype=BF),
            shaped(NT, PAD, 128, dtype=BF),
            shaped(2, seq_len, 1),
        ],
        in_specs=[SMEM_SPEC] + whole(8),
        out_specs=whole(5),
        compiler_params=BIG,
        cost_estimate=LONG,
    )(
        where,
        *far(hidden_in),
        row(ln1_gain),
        row(ln1_shift),
        *far(qkv_weight),
        row(query_bias),
        row(value_bias),
        segments,
        seg_col,
    )
    piece, ctx_send = tie(piece, ctx_send)
    ctx_got = exchange(ctx_send, T)
    beside = hop(piece, 2)
    own_w = jnp.stack(
        [jnp.where(odd == 0, piece, beside), jnp.where(odd == 0, beside, piece)], 1
    ).reshape(NT * HEAD_DIM, width)
    other_w = hop(own_w, 1)


    grad_pad = pad_rows(out_grad.astype(BF))
    gelu_in_grad = dot_nt(grad_pad, down_weight)
    hid_pad = pad_rows(hidden_in)
    out_grad_pad = pad_rows(out_grad)

    rows = 320
    tile = lambda w: pl.BlockSpec((rows, w), lambda i: (i, 0))
    fixed = lambda *shape: pl.BlockSpec(shape, lambda i: (0,) * len(shape))
    middle, act_two, gelu_low, up_low, norm_two_part, up_bias_part = pl.pallas_call(
        feed,
        grid=(PAD // rows,),
        out_shape=[
            shaped(PAD, width),
            shaped(PAD, width, dtype=BF),
            shaped(PAD, 512, dtype=BF),
            shaped(PAD, 512, dtype=BF),
            shaped(PAD, width, dtype=BF),
            shaped(1, 512),
        ],
        in_specs=[
            pl.BlockSpec((NT, rows, 128), lambda i: (0, i, 0)),
            fixed(512, width),
            fixed(512, width),
            tile(width),
            fixed(1, width),
            fixed(1, width),
            fixed(1, width),
            fixed(width, 512),
            fixed(1, 512),
            tile(512),
        ],
        out_specs=[tile(width), tile(width), tile(512), tile(512), tile(width), fixed(1, 512)],
        compiler_params=BIG,
        cost_estimate=TINY,
    )(
        *far(ctx_got, own_w, other_w, hid_pad),
        row(dense_bias),
        row(ln2_gain),
        row(ln2_shift),
        *far(up_weight),
        row(up_bias),
        *far(gelu_in_grad),
    )
    two_got = exchange(norm_two_part.reshape(NT, BLK, width), T)

    mlp_part = pl.pallas_call(
        mlp_out,
        grid=(1,),
        out_shape=shaped(NT, 2 * BLK, width, dtype=BF),
        in_specs=[fixed(PAD, 512), fixed(512, width)],
        out_specs=pl.BlockSpec((NT, BLK, width), lambda i: (0, 1, 0)),
        compiler_params=BIG,
        cost_estimate=TINY,
    )(*far(gelu_low, down_weight))
    e_keep, e_give, down_bias_part = simple_at(
        early_grads,
        [shaped(512, width, dtype=BF), shaped(512, width, dtype=BF), shaped(1, width)],
        where, act_two, up_low, grad_pad, gelu_low,
    )
    e_core = hop(e_give, 1)
    two_got, e_core, mlp_part = tie(two_got, e_core, mlp_part)

    mine = pl.BlockSpec((BLK, width), lambda i, m: (m[0], 0))
    zero = lambda *shape: pl.BlockSpec(shape, lambda i, m: (0,) * len(shape))
    back_two, branch_send, sums_two = pl.pallas_call(
        norm_two_back,
        out_shape=[shaped(BLK, width), shaped(NT, 2 * BLK, width, dtype=BF), shaped(8, width)],
        grid_spec=pltpu.PrefetchScalarGridSpec(
            num_scalar_prefetch=1,
            grid=(1,),
            in_specs=[
                zero(NT, BLK, width), mine, mine, zero(1, width),
                pl.BlockSpec(memory_space=pl.ANY),
            ],
            out_specs=[zero(BLK, width), zero(NT, BLK, width), zero(8, width)],
        ),
        input_output_aliases={5: 1},
        compiler_params=BIG,
        cost_estimate=TINY,
    )(
        me.reshape(1),
        *far(two_got, middle, out_grad_pad),
        row(ln2_gain),
        *far(mlp_part),
    )
    branch = exchange(branch_send, T)

    e_core, branch_send = tie(e_core, branch_send)
    e_own, *e_y = simple_at(
        early_core,
        [shaped(2, 64, width, dtype=BF)] * 4,
        where, e_keep.reshape(2, 4, 64, width), e_core.reshape(2, 4, 64, width),
    )
    e_y = tie(*[hop(e, 2 * (k + 1)) for k, e in enumerate(e_y)])
    e_two = sum([e.astype(F32) for e in e_y], e_own.astype(F32)).astype(BF)
    branch, e_two = tie(branch, e_two)
    e_z = hop(e_two, 8)

    qkv_grad_low, norm_one_part = pl.pallas_call(
        attend_backward,
        out_shape=[shaped(PAD, 384, dtype=BF), shaped(NT, 2 * BLK, width, dtype=BF)],
        in_specs=[SMEM_SPEC] + whole(7),
        out_specs=whole(2),
        scratch_shapes=[pltpu.VMEM((4, HEAD_DIM, PAD), F32), pltpu.VMEM((PAD, 128), BF)],
        compiler_params=BIG,
        cost_estimate=LONG,
    )(where, *far(branch, dense_weight, qkv_low, lse), segments, seg_col, *far(qkv_weight))
    norm_one_part, e_z = tie(norm_one_part, e_z)
    one_got = exchange(norm_one_part, T)

    e_three = z_add(e_two, e_z)
    e_y = y_spread(e_three)
    l_keep, l_give, vec = late_call(
        where, act_one, qkv_grad_low, branch, context, norm_one_part, hidden_in, sums_two,
        up_bias_part, down_bias_part,
    )
    l_give, *e_y = tie(l_give, *e_y)
    l_core = hop(l_give, 1)
    l_own, *l_y, vec = simple_at(
        late_core,
        [shaped(2, 80, 512, dtype=BF)] * 4 + [shaped(16, 512)],
        where, l_keep.reshape(2, 4, 64, 512), l_core, vec,
    )
    e_by_y = jnp.stack([e_three, *e_y])
    e_core, *l_y = tie(hop(e_by_y, 1), *[hop(p, 2 * (k + 1)) for k, p in enumerate(l_y)])
    l_two, vec = simple(
        late_y, [shaped(2, 80, 512, dtype=BF), shaped(16, 512)], l_own, *l_y, vec
    )
    one_got, l_two, vec, e_core, e_by_y = tie(one_got, l_two, vec, e_core, e_by_y)
    l_z = hop(l_two, 8)

    in_send = pl.pallas_call(
        norm_one_back,
        out_shape=shaped(NT, BLK + 16, width, dtype=BF),
        grid_spec=pltpu.PrefetchScalarGridSpec(
            num_scalar_prefetch=1,
            grid=(1,),
            in_specs=[
                zero(NT, BLK, width), mine, zero(BLK, width), zero(1, width), zero(16, 512)
            ],
            out_specs=zero(NT, BLK + 16, width),
        ),
        compiler_params=BIG,
        cost_estimate=LONG,
    )(me.reshape(1), *far(one_got, hid_pad, back_two), row(ln1_gain), *far(vec))
    in_send, l_z, one_got, e_core, e_by_y = tie(in_send, l_z, one_got, e_core, e_by_y)
    in_got = exchange(in_send, T)

    l_three, down_bias_grad, up_bias_grad, query_bias_grad, value_bias_grad = simple(
        late_z,
        [shaped(2, 64, 512, dtype=BF)] + [shaped(1, n) for n in (width, 512, 128, 128)],
        l_two, l_z, vec,
    )
    up_weight_grad, down_weight_grad = natural_chunks(e_by_y, e_core, dp, 512)
    block_out = pl.pallas_call(
        add_rows,
        grid=(NT // 4,),
        out_shape=shaped(seq_len, width),
        in_specs=[
            pl.BlockSpec((4 * BLK, width), lambda i: (i, 0)),
            pl.BlockSpec((4, BLK, width), lambda i: (i, 1, 0)),
            fixed(1, width),
        ],
        out_specs=pl.BlockSpec((4 * BLK, width), lambda i: (i, 0)),
        compiler_params=BIG,
        cost_estimate=SHORT,
    )(*far(middle, one_got), row(down_bias))
    up_weight_grad, block_out, *l_y = tie(up_weight_grad, block_out, *y_spread(l_three))
    l_by_y = jnp.stack([l_three, *l_y])
    l_core = hop(l_by_y, 1)
    qkv_weight_grad, dense_weight_grad = natural_chunks(l_by_y, l_core, dp, 384)
    in_got, qkv_weight_grad = tie(in_got, qkv_weight_grad)
    shared = jnp.sum(in_got[:, BLK : BLK + 8].astype(F32) + in_got[:, BLK + 8 :].astype(F32), 0)
    shared = shared + hop(shared, 8)
    input_grad = out_grad + in_got[:, :BLK].reshape(PAD, width)[:seq_len].astype(F32)
    return (
        block_out,
        input_grad,
        shared[0],
        shared[1],
        qkv_weight_grad,
        query_bias_grad[0],
        value_bias_grad[0],
        dense_weight_grad,
        shared[4],
        shared[2],
        shared[3],
        up_weight_grad,
        up_bias_grad[0],
        down_weight_grad,
        down_bias_grad[0],
    )


def solution(mesh):
    placed = (
        P("dp", None),
        P("dp", None),
        P(),
        P(),
        P(None, "tensor"),
        P("tensor"),
        P("tensor"),
        P("tensor", None),
        P(),
        P(),
        P(),
        P(None, "tensor"),
        P("tensor"),
        P("tensor", None),
        P(),
        P("dp", None),
    )
    return jax.shard_map(
        per_device,
        mesh=mesh,
        in_specs=placed,
        out_specs=(
            P("dp", None),
            P("dp", None),
            P(),
            P(),
            P(None, "tensor"),
            P("tensor"),
            P("tensor"),
            P("tensor", None),
            P(),
            P(),
            P(),
            P(None, "tensor"),
            P("tensor"),
            P("tensor", None),
            P(),
        ),
        check_vma=False,
    )
```

```python
from functools import partial

import jax
import jax.numpy as jnp
from jax import lax
from jax.experimental import pallas as pl
from jax.experimental.pallas import tpu as pltpu
from jax.sharding import PartitionSpec as P

HEADS = 16
HEAD_DIM = 64
EPS = 1e-05
NEG = -1000000000.0
T = "tensor"
DP = "dp"
NT = 8
BLK = 80
PAD = NT * BLK
BF = jnp.bfloat16
F32 = jnp.float32


def norm_stats(values_in):
    row_mean = jnp.mean(values_in, -1, keepdims=True)
    centred = values_in - row_mean
    variance = jnp.mean(centred * centred, -1, keepdims=True)
    recip = lax.rsqrt(variance + EPS)
    return centred * recip, recip


def norm_backward(grad_out, normal_part, recip, gain_vec):
    scaled = grad_out * gain_vec
    return recip * (
        scaled
        - jnp.mean(scaled, -1, keepdims=True)
        - normal_part * jnp.mean(scaled * normal_part, -1, keepdims=True)
    )


def dot(a, b):
    return jnp.dot(a, b, preferred_element_type=F32)


def dot_nt(a, b):
    return lax.dot_general(a, b, (((1,), (1,)), ((), ())), preferred_element_type=F32)


def dot_tn(a, b):
    return lax.dot_general(a, b, (((0,), (0,)), ((), ())), preferred_element_type=F32)


def pad_rows(a):
    return jnp.pad(a, ((0, PAD - a.shape[0]), (0, 0)))


def block_of(a, j):
    return lax.dynamic_slice_in_dim(a, j * BLK, BLK, 0)


def exchange(a, axis):
    return lax.all_to_all(a, axis, 0, 0, tiled=True)


def gather(piece):
    return exchange(jnp.broadcast_to(piece[None], (NT,) + piece.shape), T)


def hop(a, mask):
    return lax.ppermute(a, DP, [(i, i ^ mask) for i in range(16)])


def tensor_hop(a, mask):
    return lax.ppermute(a, T, [(i, i ^ mask) for i in range(NT)])


def pick(a, j, axis=0):
    return lax.dynamic_index_in_dim(a, j, axis, keepdims=False)


def place(dp):
    return dp % 2, (dp // 2) % 4, dp // 8


def z_add(two, got):
    return (two.astype(F32) + got.astype(F32)).astype(BF)


def y_spread(by_z):
    return tuple(hop(by_z, 2 * k) for k in (1, 2, 3))


def spread(where_ref, own_ref, other_ref, left_ref, right_ref):
    chunk = own_ref.shape[2]
    cut = left_ref.shape[1]
    core, y = where_ref[0], where_ref[1]
    for c in range(2):
        for z in range(2):
            for pair in (0, 2):
                parts = []
                for j in (pair, pair + 1):
                    a, b = own_ref[y ^ j, z], other_ref[y ^ j, z]
                    parts.append(jnp.where(core == c, a, b))
                rows = jnp.concatenate(parts, 0)
                lo = (c * 8 + z * 4 + pair) * chunk
                left_ref[lo : lo + 2 * chunk, :] = rows[:, :cut].astype(F32)
                right_ref[:, lo : lo + 2 * chunk] = jnp.transpose(rows[:, cut:]).astype(F32)


def natural_chunks(own, other, dp, cut):
    core, y, _ = place(dp)
    n, chunk, width = 16, own.shape[2], own.shape[3]
    return pl.pallas_call(
        spread,
        out_shape=[shaped(n * chunk, cut), shaped(width - cut, n * chunk)],
        in_specs=[SMEM_SPEC] + whole(2),
        out_specs=whole(2),
        compiler_params=BIG,
        cost_estimate=SHORT,
    )(jnp.stack([core, y]).astype(jnp.int32), *far(own, other))


def attend_forward(
    where_ref, hid_ref, gain_ref, shift_ref, w_ref, qb_ref, vb_ref, srow_ref, scol_ref,
    act_ref, qkv_ref, ctx_ref, send_ref, lse_ref,
):
    seq_len = hid_ref.shape[0]
    for lo, hi in row_blocks(seq_len):
        xhat, _ = norm_stats(hid_ref[lo:hi, :])
        act_ref[lo:hi, :] = (xhat * gain_ref[...] + shift_ref[...]).astype(BF)
    none = jnp.zeros((1, HEAD_DIM), F32)
    cut = HEAD_DIM
    bias = jnp.concatenate(
        [qb_ref[:, :cut], none, vb_ref[:, :cut], qb_ref[:, cut:], none, vb_ref[:, cut:]], 1
    )
    for lo, hi in halves(seq_len):
        qkv_ref[lo:hi, :] = (dot(act_ref[lo:hi, :], w_ref[...]) + bias).astype(BF)
    even = where_ref[1] == 0
    slopes = head_slopes(where_ref)
    for lo, hi in row_blocks(seq_len):
        allowed, distance = masks(lo, hi, srow_ref, scol_ref)
        outs = []
        for h in range(2):
            s = head_scores(qkv_ref, slopes, h, lo, hi, allowed, distance)
            top = jnp.max(s, -1, keepdims=True)
            e = jnp.exp(s - top)
            total = jnp.sum(e, -1, keepdims=True)
            lse_ref[h, lo:hi, :] = top + jnp.log(total)
            p = (e / total).astype(BF)
            outs.append(dot(p, qkv_ref[:hi, head_part(h, 2)]).astype(BF))
        ctx_ref[lo:hi, :] = jnp.concatenate(outs, 1)
        first = jnp.where(even, outs[0].astype(F32), outs[1].astype(F32))
        second = jnp.where(even, outs[1].astype(F32), outs[0].astype(F32))
        both = jnp.concatenate([first, second], 1).astype(BF)
        for i in range(NT):
            send_ref[i, lo:hi, :] = both
    pad = jnp.zeros((PAD - seq_len, 2 * HEAD_DIM), BF)
    for i in range(NT):
        send_ref[i, seq_len:, :] = pad


def row_blocks(n):
    return [(lo, min(lo + 128, n)) for lo in range(0, n, 128)]


def halves(n):
    return [(0, 304), (304, n)]


def head_part(h, c):
    start = (h * 3 + c) * HEAD_DIM
    return slice(start, start + HEAD_DIM)


def head_slopes(where_ref):
    first = (where_ref[0] * 2).astype(F32)
    return [
        jnp.exp2(jnp.full((1, 1), -(8.0 / HEADS), F32) * (first + (h + 1.0))) for h in range(2)
    ]


def masks(lo, hi, srow_ref, scol_ref):
    shape = (hi - lo, hi)
    diff = lax.broadcasted_iota(jnp.int32, shape, 1) - lax.broadcasted_iota(jnp.int32, shape, 0) - lo
    allowed = (diff <= 0) & (scol_ref[lo:hi, :] == srow_ref[:, :hi])
    return allowed, diff.astype(F32)


def head_scores(qkv_ref, slopes, h, lo, hi, allowed, distance):
    raw = dot_nt(qkv_ref[lo:hi, head_part(h, 0)], qkv_ref[:hi, head_part(h, 1)])
    return jnp.where(allowed, raw * HEAD_DIM ** (-0.5) + slopes[h] * distance, NEG)


def attend_backward(
    where_ref, branch_ref, wd_ref, qkv_ref, lse_ref, srow_ref, scol_ref, w_ref,
    grad_ref, part_ref, acc_ref, cg_ref,
):
    seq_len = qkv_ref.shape[0]
    scale = HEAD_DIM ** (-0.5)
    for i in (0, 4):
        rows = jnp.concatenate([branch_ref[j, :BLK, :] for j in range(i, i + 4)], 0)
        cg_ref[i * BLK : (i + 4) * BLK, :] = dot_nt(rows, wd_ref[...]).astype(BF)
    total = branch_ref[0, BLK:, :].astype(F32)
    for j in range(1, NT):
        total = total + branch_ref[j, BLK:, :].astype(F32)
    total = total.astype(BF)
    for j in range(NT):
        part_ref[j, BLK:, :] = total
    acc_ref[...] = jnp.zeros_like(acc_ref)
    slopes = head_slopes(where_ref)
    for lo, hi in row_blocks(seq_len):
        allowed, distance = masks(lo, hi, srow_ref, scol_ref)
        cg_all = cg_ref[lo:hi, :]
        for h in range(2):
            s = head_scores(qkv_ref, slopes, h, lo, hi, allowed, distance)
            p = jnp.exp(s - lse_ref[h, lo:hi, :])
            cg = cg_all[:, h * HEAD_DIM : (h + 1) * HEAD_DIM]
            pg = dot_nt(cg, qkv_ref[:hi, head_part(h, 2)])
            acc_ref[2 * h + 1, :, :hi] += dot_tn(cg, p.astype(BF))
            sg = (p * (pg - jnp.sum(pg * p, -1, keepdims=True))).astype(BF)
            grad_ref[lo:hi, head_part(h, 0)] = (
                dot(sg, qkv_ref[:hi, head_part(h, 1)]) * scale
            ).astype(BF)
            acc_ref[2 * h, :, :hi] += dot_tn(qkv_ref[lo:hi, head_part(h, 0)], sg)
    for h in range(2):
        kg = jnp.transpose(acc_ref[2 * h, :, :]) * scale
        vg = jnp.transpose(acc_ref[2 * h + 1, :, :])
        grad_ref[:, head_part(h, 1)] = kg.astype(BF)
        grad_ref[:, head_part(h, 2)] = vg.astype(BF)
    for h in range(2):
        grad_ref[seq_len:, head_part(h, 0)] = jnp.zeros((PAD - seq_len, HEAD_DIM), BF)
    for lo in range(0, PAD, 320):
        part = dot_nt(grad_ref[lo : lo + 320, :], w_ref[...]).astype(BF)
        for j in range(4):
            part_ref[lo // BLK + j, :BLK, :] = part[j * BLK : (j + 1) * BLK, :]


def feed(
    ctx_ref, own_ref, other_ref, hid_ref, db_ref, gain_ref, shift_ref, up_ref, ub_ref, gin_ref,
    mid_ref, act_ref, gelu_ref, low_ref, part_ref, sum_ref,
):
    step = pl.program_id(0)
    ctx_a = jnp.concatenate([ctx_ref[i, :, :HEAD_DIM] for i in range(NT)], 1)
    ctx_b = jnp.concatenate([ctx_ref[i, :, HEAD_DIM:] for i in range(NT)], 1)
    attn = dot(ctx_a, own_ref[...]) + dot(ctx_b, other_ref[...])
    middle = hid_ref[...] + (attn + db_ref[...])
    mid_ref[...] = middle
    xhat, _ = norm_stats(middle)
    act = (xhat * gain_ref[...] + shift_ref[...]).astype(BF)
    act_ref[...] = act
    x = dot(act, up_ref[...]) + ub_ref[...]
    a = 0.7978845608028654
    t = jnp.tanh(a * (x + 0.044715 * x * x * x))
    gelu_ref[...] = (x * (0.5 * (1.0 + t))).astype(BF)
    slope = 0.5 * (1.0 + t) + 0.5 * x * (1.0 - t * t) * (a * (1.0 + 3 * 0.044715 * x * x))
    low = (gin_ref[...] * slope).astype(BF)
    low_ref[...] = low
    part_ref[...] = dot_nt(low, up_ref[...]).astype(BF)

    @pl.when(step == 0)
    def _():
        sum_ref[...] = jnp.zeros_like(sum_ref)

    sum_ref[...] += jnp.sum(low.astype(F32), 0, keepdims=True)


def norm_two_back(
    seq_len, me_ref, got_ref, mid_ref, og_ref, gain_ref, mlp_ref, back_ref, send_ref, sum_ref
):
    total = got_ref[0].astype(F32)
    for i in range(1, NT):
        total = total + got_ref[i].astype(F32)
    xhat, recip = norm_stats(mid_ref[...])
    back = norm_backward(total, xhat, recip, gain_ref[...])
    back_ref[...] = back
    rows = me_ref[0] * BLK + lax.broadcasted_iota(jnp.int32, back.shape, 0)
    branch = jnp.where(rows < seq_len, og_ref[...] + back, 0.0).astype(BF)
    for i in range(NT):
        send_ref[i] = branch
    sum_ref[0:1, :] = jnp.sum(total * xhat, 0, keepdims=True)
    sum_ref[1:2, :] = jnp.sum(total, 0, keepdims=True)
    sum_ref[2:3, :] = jnp.sum(branch.astype(F32), 0, keepdims=True)
    sum_ref[3:8, :] = jnp.zeros((5, sum_ref.shape[1]), F32)


def norm_one_back(me_ref, got_ref, hid_ref, back_ref, gain_ref, vec_ref, send_ref):
    total = got_ref[0].astype(F32)
    for i in range(1, NT):
        total = total + got_ref[i].astype(F32)
    xhat, recip = norm_stats(hid_ref[...])
    delta = (back_ref[...] + norm_backward(total, xhat, recip, gain_ref[...])).astype(BF)
    pairs = [vec_ref[2 * i : 2 * i + 2, :] for i in range(8)]
    vec = jnp.concatenate([jnp.concatenate([p[:1], p[1:]], 1) for p in pairs], 0)
    both = jnp.concatenate(split(vec), 0)
    for i in range(NT):
        send_ref[i, :BLK, :] = delta
        send_ref[i, BLK:, :] = both


def mlp_out(gelu_ref, w_ref, out_ref):
    for lo in (0, 4):
        rows = slice(lo * BLK, (lo + 4) * BLK)
        part = dot(gelu_ref[rows, :], w_ref[...]).astype(BF)
        for j in range(4):
            out_ref[lo + j] = part[j * BLK : (j + 1) * BLK, :]


def early_grads(where_ref, act_ref, low_ref, grad_ref, gelu_ref, keep_ref, give_ref, sum_ref):
    half = keep_ref.shape[0]
    seq_len = grad_ref.shape[0]
    for ref, side in ((keep_ref, where_ref[1]), (give_ref, 1 - where_ref[1])):
        cols = pl.ds(pl.multiple_of(side * half, half), half)
        ref[:, :512] = dot_tn(act_ref[:, cols], low_ref[...]).astype(BF)
        ref[:, 512:] = dot_tn(grad_ref[:, cols].astype(BF), gelu_ref[:seq_len, :]).astype(BF)
    sum_ref[...] = jnp.sum(grad_ref[...].astype(BF).astype(F32), 0, keepdims=True)


def split(v):
    high = v.astype(BF)
    return high, (v - high.astype(F32)).astype(BF)


def join(high, low):
    return high.astype(F32) + low.astype(F32)


def late_grads(
    where_ref, act_ref, grad_ref, branch_ref, ctx_ref, part_ref, hid_ref, two_ref, up_ref,
    down_ref, keep_ref, give_ref, vec_ref,
):
    seq_len, width = act_ref.shape
    half = width // 2
    for ref, side in ((keep_ref, where_ref[1]), (give_ref, 1 - where_ref[1])):
        cols = pl.ds(pl.multiple_of(side * half, half), half)
        ref[:half, :384] = dot_tn(act_ref[:, cols], grad_ref[:seq_len, :]).astype(BF)
        branch = jnp.concatenate([branch_ref[j, :BLK, cols] for j in range(NT)], 0)
        ref[:half, 384:] = dot_tn(branch[:seq_len], ctx_ref[...]).astype(BF)
    gain = jnp.zeros((1, width), F32)
    shift = gain
    for j in range(NT):
        lo, hi = j * BLK, min(j * BLK + BLK, seq_len)
        xhat, _ = norm_stats(hid_ref[lo:hi, :])
        part = part_ref[j, : hi - lo, :].astype(F32)
        gain = gain + jnp.sum(part * xhat, 0, keepdims=True)
        shift = shift + jnp.sum(part, 0, keepdims=True)
    sums = jnp.sum(grad_ref[...].astype(F32), 0, keepdims=True)
    last = jnp.concatenate([up_ref[...], sums, jnp.zeros((1, 128), F32)], 1)
    vectors = [
        gain, shift, two_ref[0:1, :], two_ref[1:2, :], two_ref[2:3, :], down_ref[...], last,
        jnp.zeros_like(last),
    ]
    for i, v in enumerate(vectors):
        vec_ref[2 * i : 2 * i + 1, :] = v[:, :half]
        vec_ref[2 * i + 1 : 2 * i + 2, :] = v[:, half:]
    high, low = split(vec_ref[...])
    give_ref[half : half + 16, :] = high
    give_ref[half + 16 :, :] = low


def early_core(where_ref, keep_ref, got_ref, own_ref, one_ref, two_ref, three_ref):
    y = where_ref[2]
    for k, ref in enumerate((own_ref, one_ref, two_ref, three_ref)):
        for z in range(2):
            total = keep_ref[z, y ^ k].astype(F32) + got_ref[z, y ^ k].astype(F32)
            ref[z] = total.astype(BF)


def late_core(
    where_ref, keep_ref, got_ref, vec_ref, own_ref, one_ref, two_ref, three_ref, out_ref
):
    y = where_ref[2]
    chunk = keep_ref.shape[2]
    half = 8 * chunk
    vec = vec_ref[...] + join(got_ref[half : half + 16, :], got_ref[half + 16 :, :])
    out_ref[...] = vec
    parts = split(vec)
    for k, ref in enumerate((own_ref, one_ref, two_ref, three_ref)):
        for z in range(2):
            rows = pl.ds(pl.multiple_of((z * 4 + (y ^ k)) * chunk, chunk), chunk)
            total = keep_ref[z, y ^ k].astype(F32) + got_ref[rows, :].astype(F32)
            ref[z, :chunk, :] = total.astype(BF)
            ref[z, chunk:, :] = parts[z]


def late_y(own_ref, one_ref, two_ref, three_ref, vec_ref, out_ref, sum_ref):
    chunk = own_ref.shape[1] - 16
    vec = vec_ref[...]
    for ref in (one_ref, two_ref, three_ref):
        vec = vec + join(ref[0, chunk:, :], ref[1, chunk:, :])
    sum_ref[...] = vec
    parts = split(vec)
    for z in range(2):
        total = own_ref[z, :chunk, :].astype(F32)
        for ref in (one_ref, two_ref, three_ref):
            total = total + ref[z, :chunk, :].astype(F32)
        out_ref[z, :chunk, :] = total.astype(BF)
        out_ref[z, chunk:, :] = parts[z]


def late_z(own_ref, got_ref, vec_ref, out_ref, down_ref, up_ref, query_ref, value_ref):
    chunk = out_ref.shape[1]
    vec = vec_ref[...] + join(got_ref[0, chunk:, :], got_ref[1, chunk:, :])
    down_ref[...] = jnp.concatenate([vec[10:11], vec[11:12]], 1)
    up_ref[...] = vec[12:13]
    for ref, c in ((query_ref, 0), (value_ref, 2)):
        ref[...] = jnp.concatenate([vec[13:14, head_part(h, c)] for h in range(2)], 1)
    for z in range(2):
        total = own_ref[z, :chunk, :].astype(F32) + got_ref[z, :chunk, :].astype(F32)
        out_ref[z] = total.astype(BF)


def add_rows(mid_ref, got_ref, bias_ref, out_ref):
    for i in range(got_ref.shape[0]):
        rows = slice(i * BLK, (i + 1) * BLK)
        out_ref[rows, :] = mid_ref[rows, :] + (got_ref[i].astype(F32) + bias_ref[...])


def simple(kernel, outs, *args):
    return pl.pallas_call(
        kernel,
        out_shape=outs,
        in_specs=whole(len(args)),
        out_specs=whole(len(outs)),
        compiler_params=BIG,
        cost_estimate=TINY,
    )(*far(*args))


def late_call(where, *args):
    first = pl.BlockSpec((NT, BLK, 1024), lambda i: (0, 0, 0))
    full = lambda a: pl.BlockSpec(a.shape, lambda i: (0, 0))
    outs = [shaped(512, 512, dtype=BF), shaped(544, 512, dtype=BF), shaped(16, 512)]
    return pl.pallas_call(
        late_grads,
        grid=(1,),
        out_shape=outs,
        in_specs=[SMEM_SPEC] + [first if a.ndim == 3 else full(a) for a in args],
        out_specs=[pl.BlockSpec(o.shape, lambda i: (0, 0)) for o in outs],
        compiler_params=BIG,
        cost_estimate=LONG,
    )(where, *far(*args))


def simple_at(kernel, outs, where, *args, cost=None):
    return pl.pallas_call(
        kernel,
        out_shape=outs,
        in_specs=[SMEM_SPEC] + whole(len(args)),
        out_specs=whole(len(outs)),
        compiler_params=BIG,
        cost_estimate=cost or TINY,
    )(where, *far(*args))


def whole(n):
    return [pl.BlockSpec(memory_space=pltpu.VMEM)] * n


SMEM_SPEC = pl.BlockSpec(memory_space=pltpu.SMEM)
LONG = pl.CostEstimate(flops=4 << 30, bytes_accessed=24 << 20, transcendentals=0)
SHORT = pl.CostEstimate(flops=1 << 20, bytes_accessed=10 << 20, transcendentals=0)
TINY = pl.CostEstimate(flops=1, bytes_accessed=1, transcendentals=0)
BIG = pltpu.CompilerParams(vmem_limit_bytes=40 << 20)


def shaped(*shape, dtype=F32):
    return pltpu.HBM(shape, dtype)


def far(*arrays):
    return [pltpu.with_memory_space_constraint(a, pltpu.HBM) for a in arrays]


def tie(*arrays):
    return lax.optimization_barrier(arrays)


def per_device(
    hidden_in,
    segments,
    ln1_gain,
    ln1_shift,
    qkv_weight,
    query_bias,
    value_bias,
    dense_weight,
    dense_bias,
    ln2_gain,
    ln2_shift,
    up_weight,
    up_bias,
    down_weight,
    down_bias,
    out_grad,
):
    seq_len, width = hidden_in.shape
    me = lax.axis_index(T)
    dp = lax.axis_index(DP)
    core = dp % 2
    row = lambda v: v.reshape(1, -1)
    where = jnp.stack([me, core, (dp // 2) % 4]).astype(jnp.int32)

    part = HEAD_DIM // 2
    odd = (dp // 2) % 2
    piece = lax.dynamic_slice_in_dim(dense_weight, core * HEAD_DIM + odd * part, part, 0)
    piece = gather(piece)

    seg_col = segments.reshape(seq_len, 1)
    act_one, qkv_low, context, ctx_send, lse = pl.pallas_call(
        attend_forward,
        out_shape=[
            shaped(seq_len, width, dtype=BF),
            shaped(seq_len, 384, dtype=BF),
            shaped(seq_len, 128, dtype=BF),
            shaped(NT, PAD, 128, dtype=BF),
            shaped(2, seq_len, 1),
        ],
        in_specs=[SMEM_SPEC] + whole(8),
        out_specs=whole(5),
        compiler_params=BIG,
        cost_estimate=LONG,
    )(
        where,
        *far(hidden_in),
        row(ln1_gain),
        row(ln1_shift),
        *far(qkv_weight),
        row(query_bias),
        row(value_bias),
        segments,
        seg_col,
    )
    piece, ctx_send = tie(piece, ctx_send)
    ctx_got = exchange(ctx_send, T)
    beside = hop(piece, 2)
    own_w = jnp.stack(
        [jnp.where(odd == 0, piece, beside), jnp.where(odd == 0, beside, piece)], 1
    ).reshape(NT * HEAD_DIM, width)
    other_w = hop(own_w, 1)


    grad_pad = pad_rows(out_grad.astype(BF))
    gelu_in_grad = dot_nt(grad_pad, down_weight)
    hid_pad = pad_rows(hidden_in)

    rows = 320
    tile = lambda w: pl.BlockSpec((rows, w), lambda i: (i, 0))
    fixed = lambda *shape: pl.BlockSpec(shape, lambda i: (0,) * len(shape))
    middle, act_two, gelu_low, up_low, norm_two_part, up_bias_part = pl.pallas_call(
        feed,
        grid=(PAD // rows,),
        out_shape=[
            shaped(PAD, width),
            shaped(PAD, width, dtype=BF),
            shaped(PAD, 512, dtype=BF),
            shaped(PAD, 512, dtype=BF),
            shaped(PAD, width, dtype=BF),
            shaped(1, 512),
        ],
        in_specs=[
            pl.BlockSpec((NT, rows, 128), lambda i: (0, i, 0)),
            fixed(512, width),
            fixed(512, width),
            tile(width),
            fixed(1, width),
            fixed(1, width),
            fixed(1, width),
            fixed(width, 512),
            fixed(1, 512),
            tile(512),
        ],
        out_specs=[tile(width), tile(width), tile(512), tile(512), tile(width), fixed(1, 512)],
        compiler_params=BIG,
        cost_estimate=TINY,
    )(
        *far(ctx_got, own_w, other_w, hid_pad),
        row(dense_bias),
        row(ln2_gain),
        row(ln2_shift),
        *far(up_weight),
        row(up_bias),
        *far(gelu_in_grad),
    )
    two_got = exchange(norm_two_part.reshape(NT, BLK, width), T)

    mlp_part = pl.pallas_call(
        mlp_out,
        grid=(1,),
        out_shape=shaped(NT, 2 * BLK, width, dtype=BF),
        in_specs=[fixed(PAD, 512), fixed(512, width)],
        out_specs=pl.BlockSpec((NT, BLK, width), lambda i: (0, 1, 0)),
        compiler_params=BIG,
        cost_estimate=TINY,
    )(*far(gelu_low, down_weight))
    e_keep, e_give, down_bias_part = simple_at(
        early_grads,
        [shaped(512, width, dtype=BF), shaped(512, width, dtype=BF), shaped(1, width)],
        where, act_two, up_low, out_grad, gelu_low,
    )
    e_core = hop(e_give, 1)
    two_got, e_core, mlp_part = tie(two_got, e_core, mlp_part)

    mine = pl.BlockSpec((BLK, width), lambda i, m: (m[0], 0))
    zero = lambda *shape: pl.BlockSpec(shape, lambda i, m: (0,) * len(shape))
    back_two, branch_send, sums_two = pl.pallas_call(
        partial(norm_two_back, seq_len),
        out_shape=[shaped(BLK, width), shaped(NT, 2 * BLK, width, dtype=BF), shaped(8, width)],
        grid_spec=pltpu.PrefetchScalarGridSpec(
            num_scalar_prefetch=1,
            grid=(1,),
            in_specs=[
                zero(NT, BLK, width), mine, mine, zero(1, width),
                pl.BlockSpec(memory_space=pl.ANY),
            ],
            out_specs=[zero(BLK, width), zero(NT, BLK, width), zero(8, width)],
        ),
        input_output_aliases={5: 1},
        compiler_params=BIG,
        cost_estimate=TINY,
    )(
        me.reshape(1),
        *far(two_got, middle, out_grad),
        row(ln2_gain),
        *far(mlp_part),
    )
    branch = exchange(branch_send, T)

    e_core, branch_send = tie(e_core, branch_send)
    e_own, *e_y = simple_at(
        early_core,
        [shaped(2, 64, width, dtype=BF)] * 4,
        where, e_keep.reshape(2, 4, 64, width), e_core.reshape(2, 4, 64, width),
    )
    e_y = tie(*[hop(e, 2 * (k + 1)) for k, e in enumerate(e_y)])
    e_two = sum([e.astype(F32) for e in e_y], e_own.astype(F32)).astype(BF)
    branch, e_two = tie(branch, e_two)
    e_z = hop(e_two, 8)

    qkv_grad_low, norm_one_part = pl.pallas_call(
        attend_backward,
        out_shape=[shaped(PAD, 384, dtype=BF), shaped(NT, 2 * BLK, width, dtype=BF)],
        in_specs=[SMEM_SPEC] + whole(7),
        out_specs=whole(2),
        scratch_shapes=[pltpu.VMEM((4, HEAD_DIM, PAD), F32), pltpu.VMEM((PAD, 128), BF)],
        compiler_params=BIG,
        cost_estimate=LONG,
    )(where, *far(branch, dense_weight, qkv_low, lse), segments, seg_col, *far(qkv_weight))
    norm_one_part, e_z = tie(norm_one_part, e_z)
    one_got = exchange(norm_one_part, T)

    e_three = z_add(e_two, e_z)
    e_y = y_spread(e_three)
    l_keep, l_give, vec = late_call(
        where, act_one, qkv_grad_low, branch, context, norm_one_part, hidden_in, sums_two,
        up_bias_part, down_bias_part,
    )
    l_give, *e_y = tie(l_give, *e_y)
    l_core = hop(l_give, 1)
    l_own, *l_y, vec = simple_at(
        late_core,
        [shaped(2, 80, 512, dtype=BF)] * 4 + [shaped(16, 512)],
        where, l_keep.reshape(2, 4, 64, 512), l_core, vec,
    )
    e_by_y = jnp.stack([e_three, *e_y])
    e_core, *l_y = tie(hop(e_by_y, 1), *[hop(p, 2 * (k + 1)) for k, p in enumerate(l_y)])
    l_two, vec = simple(
        late_y, [shaped(2, 80, 512, dtype=BF), shaped(16, 512)], l_own, *l_y, vec
    )
    one_got, l_two, vec, e_core, e_by_y = tie(one_got, l_two, vec, e_core, e_by_y)
    l_z = hop(l_two, 8)

    in_send = pl.pallas_call(
        norm_one_back,
        out_shape=shaped(NT, BLK + 16, width, dtype=BF),
        grid_spec=pltpu.PrefetchScalarGridSpec(
            num_scalar_prefetch=1,
            grid=(1,),
            in_specs=[
                zero(NT, BLK, width), mine, zero(BLK, width), zero(1, width), zero(16, 512)
            ],
            out_specs=zero(NT, BLK + 16, width),
        ),
        compiler_params=BIG,
        cost_estimate=LONG,
    )(me.reshape(1), *far(one_got, hid_pad, back_two), row(ln1_gain), *far(vec))
    in_send, l_z, one_got, e_core, e_by_y = tie(in_send, l_z, one_got, e_core, e_by_y)
    in_got = exchange(in_send, T)

    l_three, down_bias_grad, up_bias_grad, query_bias_grad, value_bias_grad = simple(
        late_z,
        [shaped(2, 64, 512, dtype=BF)] + [shaped(1, n) for n in (width, 512, 128, 128)],
        l_two, l_z, vec,
    )
    up_weight_grad, down_weight_grad = natural_chunks(e_by_y, e_core, dp, 512)
    block_out = pl.pallas_call(
        add_rows,
        grid=(NT // 4,),
        out_shape=shaped(seq_len, width),
        in_specs=[
            pl.BlockSpec((4 * BLK, width), lambda i: (i, 0)),
            pl.BlockSpec((4, BLK, width), lambda i: (i, 1, 0)),
            fixed(1, width),
        ],
        out_specs=pl.BlockSpec((4 * BLK, width), lambda i: (i, 0)),
        compiler_params=BIG,
        cost_estimate=SHORT,
    )(*far(middle, one_got), row(down_bias))
    up_weight_grad, block_out, *l_y = tie(up_weight_grad, block_out, *y_spread(l_three))
    l_by_y = jnp.stack([l_three, *l_y])
    l_core = hop(l_by_y, 1)
    qkv_weight_grad, dense_weight_grad = natural_chunks(l_by_y, l_core, dp, 384)
    in_got, qkv_weight_grad = tie(in_got, qkv_weight_grad)
    shared = jnp.sum(in_got[:, BLK : BLK + 8].astype(F32) + in_got[:, BLK + 8 :].astype(F32), 0)
    shared = shared + hop(shared, 8)
    input_grad = out_grad + in_got[:, :BLK].reshape(PAD, width)[:seq_len].astype(F32)
    return (
        block_out,
        input_grad,
        shared[0],
        shared[1],
        qkv_weight_grad,
        query_bias_grad[0],
        value_bias_grad[0],
        dense_weight_grad,
        shared[4],
        shared[2],
        shared[3],
        up_weight_grad,
        up_bias_grad[0],
        down_weight_grad,
        down_bias_grad[0],
    )


def solution(mesh):
    placed = (
        P("dp", None),
        P("dp", None),
        P(),
        P(),
        P(None, "tensor"),
        P("tensor"),
        P("tensor"),
        P("tensor", None),
        P(),
        P(),
        P(),
        P(None, "tensor"),
        P("tensor"),
        P("tensor", None),
        P(),
        P("dp", None),
    )
    return jax.shard_map(
        per_device,
        mesh=mesh,
        in_specs=placed,
        out_specs=(
            P("dp", None),
            P("dp", None),
            P(),
            P(),
            P(None, "tensor"),
            P("tensor"),
            P("tensor"),
            P("tensor", None),
            P(),
            P(),
            P(),
            P(None, "tensor"),
            P("tensor"),
            P("tensor", None),
            P(),
        ),
        check_vma=False,
    )
```
